256 devices in a mesh: tgt: 16 (over y, x), src: 8 (over z_lo, core), head: 2 (over z_hi).
Axes of the slice: x: 4, y: 4, z: 8 (z_hi: 2, z_lo: 4; z = z_hi * 4 + z_lo), core: 2. Of those that a mesh axis runs over, the one named last changes fastest.
Arguments:
- queries: bfloat16 [8192, 4096], P(('tgt', 'src'), 'head'), may hold values from -84 to 84
- keys: bfloat16 [4096, 4096], P(('src', 'tgt'), 'head'), may hold values from -3 to 3
- values: bfloat16 [4096, 4096], P(('src', 'tgt'), 'head'), may hold values from -6 to 6
- out_grad: bfloat16 [8192, 4096], P(('tgt', 'src'), 'head'), may hold values from -4 to 4
- read_points: int32 [8192], P('tgt'), may hold values from 1 to 4096, as said below
- block_mask: int32 [64, 32], replicated, may hold values from 0 to 1, as said below
Outputs:
- query_grad: bfloat16 [8192, 4096], P(('tgt', 'src'), 'head')
- key_grad: bfloat16 [4096, 4096], P(('src', 'tgt'), 'head')
- value_grad: bfloat16 [4096, 4096], P(('src', 'tgt'), 'head')
The draws below stay inside these ranges and needn't reach their ends.
Inputs may be any that keep to these rules, and one draw needn't show every extreme that they name: `read_points`: nondecreasing along the target positions; the first is 1 and the last is 4096. `block_mask`: every entry of column 0 is 1.
All inputs are finite; a program needn't handle non-finite values.
Results may differ from the reference program's by a relative error of at most 0.015.
Values may be sent and summed in bfloat16 or wider, within the bound.
No kernel may reach another device: no remote copies, remote signals or barrier semaphores. Data moves between devices by JAX's collectives and lax.ppermute only.
A program may use at most 128 MiB of HBM per device.

```python
import jax
import jax.numpy as jnp
from jax import lax

HEADS = 32
HEAD_DIM = 128
SK_DEV = 512
TILE = 128
TGT = 8192
SRC = 4096
N_SRC = 8


def base_keys(key):
    return jnp.clip(jax.random.normal(key, (SRC, HEADS * HEAD_DIM), jnp.float32), -3.0, 3.0)


def draw_keys(key, part):
    shared = base_keys(key)
    return shared.astype(jnp.bfloat16)


def draw_queries(key, part):
    key = jax.random.fold_in(key, 5)
    drawn = jnp.clip(jax.random.normal(key, (TGT, HEADS * HEAD_DIM), jnp.float32), -3.0, 3.0)
    return drawn.astype(jnp.bfloat16)


def draw_read_points(key, part):
    key = jax.random.fold_in(key, 11)
    advance = jax.random.randint(key, (TGT,), 0, 3).astype(jnp.int32)
    advance = advance.at[0].set(0)
    climb = jnp.cumsum(advance).astype(jnp.int32)
    overall = jnp.maximum(climb[-1], 1)
    return (1 + climb * (SRC - 1) // overall).astype(jnp.int32)


def draw_block_mask(key, part):
    key = jax.random.fold_in(key, 13)
    flags = (jax.random.randint(key, (TGT // TILE, SRC // TILE), 0, 4) > 0).astype(jnp.int32)
    return flags.at[:, 0].set(1)


def level_of(own_key, dims, shards, smallest, largest):
    def one(dim, shards_of):
        steps = jax.random.uniform(jax.random.fold_in(jax.random.fold_in(own_key, 6), dim), (shards_of,), jnp.float32, smallest / len(shards), largest / len(shards))
        return jnp.repeat(jnp.exp(steps), dims[dim] // shards_of).reshape((-1,) + (1,) * (len(dims) - dim - 1))

    level = one(*shards[0])
    for cut in shards[1:]:
        level = level * one(*cut)
    return level


def normal_values(rng, shape, spread, most, cuts=(), kind=jnp.bfloat16):
    loudness = level_of(rng, shape, cuts, -0.22, 0.18) if cuts else 1.0
    result = jax.random.normal(rng, shape, jnp.float32) * spread * loudness
    return jnp.minimum(jnp.maximum(result, -most), most).astype(kind)


def setup_inputs(seed: int = 0) -> dict:
    splits = jax.random.split(jax.random.key(seed), 7)
    return {
        "queries": draw_queries(jax.random.fold_in(splits[6], 71), 0),
        "keys": draw_keys(jax.random.fold_in(splits[6], 71), 0),
        "values": normal_values(splits[2], (SRC, HEADS * HEAD_DIM), 1.0, 6.0, ((0, 128), (1, 2))),
        "out_grad": normal_values(splits[3], (TGT, HEADS * HEAD_DIM), 0.25, 4.0, ((0, 128), (1, 2))),
        "read_points": draw_read_points(jax.random.fold_in(splits[6], 71), 0),
        "block_mask": draw_block_mask(jax.random.fold_in(splits[6], 71), 0),
    }


MASKED_SCORE = -1e30


def reference(queries, keys, values, out_grad, read_points, block_mask):
    softmax_scale = float(HEAD_DIM) ** -0.5
    target_pos = jnp.arange(TGT, dtype=jnp.int32)
    source_pos = jnp.arange(SRC, dtype=jnp.int32)
    tile_flags = block_mask[target_pos // TILE][:, source_pos // TILE] == 1
    allowed = (source_pos[None, :] < read_points[:, None]) & tile_flags

    def by_head(tensor):
        return tensor.reshape(tensor.shape[0], HEADS, HEAD_DIM).transpose(1, 0, 2)

    def one_head(head_args):
        query_head, key_head, value_head, grad_head = head_args
        logits = jnp.dot(query_head, key_head.T, preferred_element_type=jnp.float32) * softmax_scale
        logits = jnp.where(allowed, logits, MASKED_SCORE)
        row_max = jnp.max(logits, axis=1, keepdims=True)
        weights = jnp.where(allowed, jnp.exp(logits - row_max), 0.0)
        probs = weights / jnp.sum(weights, axis=1, keepdims=True)
        grad_prob = jnp.dot(grad_head, value_head.T, preferred_element_type=jnp.float32)
        delta_rows = jnp.sum(probs * grad_prob, axis=1, keepdims=True)
        grad_logit = probs * (grad_prob - delta_rows)
        probs_low = probs.astype(jnp.bfloat16)
        grad_low = grad_logit.astype(jnp.bfloat16)
        pieces = jnp.einsum("tjs,jsd->jtd", grad_low.reshape(TGT, N_SRC, SK_DEV).astype(jnp.float32), key_head.reshape(N_SRC, SK_DEV, HEAD_DIM).astype(jnp.float32)) * softmax_scale
        pieces = lax.optimization_barrier(pieces.astype(jnp.bfloat16))
        query_grad = jnp.sum(pieces.astype(jnp.float32), axis=0).astype(jnp.bfloat16)
        key_grad = (jnp.dot(grad_low.T, query_head, preferred_element_type=jnp.float32) * softmax_scale).astype(jnp.bfloat16)
        value_grad = jnp.dot(probs_low.T, grad_head, preferred_element_type=jnp.float32).astype(jnp.bfloat16)
        return query_grad, key_grad, value_grad

    query_heads, key_heads, value_heads = lax.map(one_head, (by_head(queries), by_head(keys), by_head(values), by_head(out_grad)))

    def merge_heads(tensor):
        return tensor.transpose(1, 0, 2).reshape(tensor.shape[1], HEADS * HEAD_DIM)

    return merge_heads(query_heads), merge_heads(key_heads), merge_heads(value_heads)
```

```python
import functools

import jax
import jax.numpy as jnp
from jax import lax
from jax.experimental import pallas as pl
from jax.experimental.pallas import tpu as pltpu
from jax.sharding import PartitionSpec as P

DIM = 128
TILE = 128
CHUNK = 512
TILES = 16
PAIRS = TILES // 2
WIDE = 2 * TILE
ROWS = TILES * TILE
HALF = TILE // 2
MASKED = -1e30
FLOOR = -1e29
SCALE = float(DIM) ** -0.5
LOG2E = 1.4426950408889634
CHUNKS = 4
NT = (((1,), (1,)), ((), ()))
LIMIT = 48 * 1024 * 1024


def dot_nt(a, b):
    return lax.dot_general(a, b, NT, preferred_element_type=jnp.float32)


def dot_nn(a, b):
    return jnp.dot(a, b, preferred_element_type=jnp.float32)


def pair_rows(own, other, pair, low):
    parts = []
    for half in range(2):
        for ref in (own, other):
            parts.append(ref[2 * pair + half, low : low + HALF, :])
    return jnp.concatenate(parts, axis=0)


def sub_rows(kv, j, low):
    return kv[4 * j : 4 * j + 4, low : low + 32, :].reshape(TILE, DIM)


def masked_scores(kv, lim, chunk, j, x, lanes, steps):
    scores = dot_nt(sub_rows(kv, j, 0), x) * (SCALE * LOG2E)
    return jnp.where(steps < lim[4 * chunk + j, lanes][None, :], scores, MASKED)


def stats_kernel(first, lim, own, other, kv0, kv1, kv2, kv3, out):
    kvs = (kv0, kv1, kv2, kv3)
    steps = lax.broadcasted_iota(jnp.int32, (TILE, WIDE), 0)
    out[...] = jnp.zeros_like(out)
    out[0:1, :] = jnp.full((1, ROWS), MASKED, jnp.float32)
    for chunk in range(CHUNKS):
        kv = kvs[chunk]

        def unit(pair, carry):
            lanes = pl.ds(pl.multiple_of(pair * WIDE, WIDE), WIDE)
            x = pair_rows(own, other, pair, 0)
            g = pair_rows(own, other, pair, HALF)
            scores = [masked_scores(kv, lim, chunk, j, x, lanes, steps) for j in range(4)]
            top = functools.reduce(jnp.maximum, scores).max(axis=0, keepdims=True)
            old = out[0:1, lanes]
            high = jnp.maximum(old, top)
            base = jnp.maximum(high, FLOOR)
            total = jnp.zeros((1, WIDE), jnp.float32)
            mixed = jnp.zeros((1, WIDE), jnp.float32)
            for j in range(4):
                weights = jnp.exp2(scores[j] - base)
                prods = dot_nt(sub_rows(kv, j, 32), g)
                total += weights.sum(axis=0, keepdims=True)
                mixed += (weights * prods).sum(axis=0, keepdims=True)
            fade = jnp.exp2(old - high)
            out[0:1, lanes] = high
            out[1:2, lanes] = out[1:2, lanes] * fade + total
            out[2:3, lanes] = out[2:3, lanes] * fade + mixed
            return carry

        lax.fori_loop(first[chunk], PAIRS, unit, 0)


def grads_kernel(chunks, start, end, *refs):
    first, lim, own, other, mine, theirs = refs[:6]
    refs = refs[6:]
    kvs, refs = refs[: len(chunks)], refs[len(chunks) :]
    if not start:
        query_in, refs = refs[0], refs[1:]
    outs, refs = refs[: len(chunks)], refs[len(chunks) :]
    if end:
        keep, send, query_acc, refs = refs[0], refs[1], refs[2], refs[3:]
    else:
        query_acc, refs = refs[0], refs[1:]
    shift, delta, key_acc, value_acc, key_t = refs
    steps = lax.broadcasted_iota(jnp.int32, (TILE, WIDE), 0)
    for tile in range(TILES):
        lanes = slice(tile * TILE, (tile + 1) * TILE)
        a = mine[:, lanes]
        b = pltpu.roll(theirs[:, lanes], HALF, 1)
        high = jnp.maximum(a[0:1], b[0:1])
        wa = jnp.exp2(a[0:1] - high)
        wb = jnp.exp2(b[0:1] - high)
        total = a[1:2] * wa + b[1:2] * wb
        mixed = a[2:3] * wa + b[2:3] * wb
        shift[0:1, lanes] = high + jnp.log2(total)
        delta[0:1, lanes] = mixed / total
    if start:
        query_acc[...] = jnp.zeros_like(query_acc)
    else:
        query_acc[...] = query_in[...]
    for index, chunk in enumerate(chunks):
        kv = kvs[index]
        for j in range(4):
            block = sub_rows(kv, j, 0).astype(jnp.float32)
            key_t[:, j * TILE : (j + 1) * TILE] = block.T.astype(jnp.bfloat16)
        key_acc[...] = jnp.zeros_like(key_acc)
        value_acc[...] = jnp.zeros_like(value_acc)

        def unit(pair, carry):
            lanes = pl.ds(pl.multiple_of(pair * WIDE, WIDE), WIDE)
            x = pair_rows(own, other, pair, 0)
            g = pair_rows(own, other, pair, HALF)
            base = shift[0:1, lanes]
            center = delta[0:1, lanes]
            lows = []
            for j in range(4):
                rows = slice(j * TILE, (j + 1) * TILE)
                scores = masked_scores(kv, lim, chunk, j, x, lanes, steps)
                probs = jnp.exp2(scores - base)
                prods = dot_nt(sub_rows(kv, j, 32), g)
                low = (probs * (prods - center)).astype(jnp.bfloat16)
                value_acc[rows, :] += dot_nn(probs.astype(jnp.bfloat16), g)
                key_acc[rows, :] += dot_nn(low, x)
                lows.append(low)
            query_acc[:, lanes] += dot_nn(key_t[...], jnp.concatenate(lows, axis=0))
            return carry

        lax.fori_loop(first[chunk], PAIRS, unit, 0)
        out = outs[index]
        out[:, 0:32, :] = (key_acc[...] * SCALE).astype(jnp.bfloat16).reshape(TILES, 32, DIM)
        out[:, 32:64, :] = value_acc[...].astype(jnp.bfloat16).reshape(TILES, 32, DIM)
    if end:
        for tile in range(TILES):
            block = query_acc[:, tile * TILE : (tile + 1) * TILE].T * SCALE
            keep[tile] = block[0:HALF]
            send[tile] = block[HALF:TILE].astype(jnp.bfloat16)


SMEM = pl.BlockSpec(memory_space=pltpu.SMEM)
VMEM = pl.BlockSpec(memory_space=pltpu.VMEM)
PARAMS = pltpu.CompilerParams(vmem_limit_bytes=LIMIT)


def cost(units, dots):
    flops = units * dots * 2 * CHUNK * WIDE * DIM
    return pl.CostEstimate(flops=flops, bytes_accessed=4 * 2**20, transcendentals=units * CHUNK * WIDE)


def row_stats(first, lim, own, other, kvs):
    return pl.pallas_call(
        stats_kernel,
        out_shape=jax.ShapeDtypeStruct((8, ROWS), jnp.float32),
        in_specs=[SMEM] + [VMEM] * 7,
        out_specs=VMEM,
        compiler_params=PARAMS,
        cost_estimate=cost(20, 4),
        name="stats",
    )(first, lim, own, other, *kvs)


def chunk_grads(chunks, start, end, first, lim, own, other, mine, theirs, kvs, query_in):
    piece = jax.ShapeDtypeStruct((TILES, 64, DIM), jnp.bfloat16)
    shapes = [piece] * len(chunks)
    scratch = [
        pltpu.VMEM((8, ROWS), jnp.float32),
        pltpu.VMEM((8, ROWS), jnp.float32),
        pltpu.VMEM((CHUNK, DIM), jnp.float32),
        pltpu.VMEM((CHUNK, DIM), jnp.float32),
        pltpu.VMEM((DIM, CHUNK), jnp.bfloat16),
    ]
    accumulator = (DIM, ROWS)
    if end:
        shapes += [jax.ShapeDtypeStruct((TILES, HALF, DIM), jnp.float32), piece]
        scratch = [pltpu.VMEM(accumulator, jnp.float32)] + scratch
    else:
        shapes += [jax.ShapeDtypeStruct(accumulator, jnp.float32)]
    operands = [first, lim, own, other, mine, theirs] + [kvs[c] for c in chunks]
    if not start:
        operands.append(query_in)
    return pl.pallas_call(
        functools.partial(grads_kernel, chunks, start, end),
        out_shape=shapes,
        in_specs=[SMEM] + [VMEM] * (len(operands) - 1),
        out_specs=[VMEM] * len(shapes),
        scratch_shapes=scratch,
        compiler_params=PARAMS,
        cost_estimate=cost(5 * len(chunks), 5),
        name="grads",
    )(*operands)


def shards(queries, keys, values, out_grad, read_points, block_mask):
    place = lax.axis_index("src")
    level, core = place // 2, place % 2

    def swap(a, mask):
        return lax.ppermute(a, "src", [(i, i ^ mask) for i in range(8)])

    def by_head(a):
        return lax.all_to_all(a, "tgt", 1, 0, tiled=True).reshape(TILES, a.shape[0], DIM)

    kv = by_head(jnp.concatenate([keys, values], axis=0))
    reads = lax.dynamic_slice_in_dim(read_points, level * TILE, TILE)
    digits = jnp.stack([reads // 64, reads % 64]).astype(jnp.bfloat16)
    digits = jnp.pad(jnp.tile(digits, (1, TILES)), ((0, 14), (0, 0)))
    packed = jnp.concatenate([queries, out_grad, digits], axis=0)
    packed, kv = lax.optimization_barrier((packed, kv))
    kvs = [kv] + [swap(kv, 2 * k) for k in range(1, CHUNKS)]
    own = by_head(packed)
    other = swap(own, 1)

    reads = own[:, 2 * HALF, :].astype(jnp.int32) * 64 + own[:, 2 * HALF + 1, :].astype(jnp.int32)
    owners = jnp.stack([level ^ k for k in range(CHUNKS)])
    starts = (owners * 2 + core) * CHUNK
    first = jnp.sum(reads[1::2, -1][None, :] <= starts[:, None], axis=1).astype(jnp.int32)
    ordered = jnp.where(core == 0, reads, jnp.roll(reads, HALF, axis=1))
    flags = block_mask.reshape(TILES, CHUNKS, CHUNKS, 2, 4)
    flags = lax.dynamic_index_in_dim(flags, level, 1, False)
    flags = lax.dynamic_index_in_dim(flags, core, 2, False)
    flags = jnp.stack([lax.dynamic_index_in_dim(flags, level ^ k, 1, False) for k in range(CHUNKS)])
    flags = flags.transpose(0, 2, 1)
    begins = starts[:, None] + TILE * jnp.arange(4, dtype=jnp.int32)[None, :]
    lim = jnp.where(flags[..., None] == 1, ordered[None, None], 0) - begins[:, :, None, None]
    lim = lim.reshape(TILES, ROWS)

    mine = row_stats(first, lim, own, other, kvs)
    theirs = swap(mine, 1)
    common = (first, lim, own, other, mine, theirs, kvs)
    part3, query_acc = chunk_grads((3,), True, False, *common, None)
    got3 = swap(part3, 6)
    part2, query_acc = chunk_grads((2,), False, False, *common, query_acc)
    got2 = swap(part2, 4)
    part1, part0, keep, send = chunk_grads((1, 0), False, True, *common, query_acc)
    got1 = swap(part1, 2)
    query = keep + swap(send, 1).astype(jnp.float32)
    sums = functools.reduce(jnp.add, [p.astype(jnp.float32) for p in (part0, got1, got2, got3)])
    result = jnp.concatenate([query, sums], axis=1).astype(jnp.bfloat16)
    result = lax.all_to_all(result, "tgt", 0, 0, tiled=True)
    result = result.transpose(1, 0, 2).reshape(128, TILES * DIM)
    return result[0:64], result[64:96], result[96:128]


def solution(mesh):
    in_specs = (
        P(("tgt", "src"), "head"),
        P(("src", "tgt"), "head"),
        P(("src", "tgt"), "head"),
        P(("tgt", "src"), "head"),
        P("tgt"),
        P(),
    )
    out_specs = (P(("tgt", "src"), "head"), P(("src", "tgt"), "head"), P(("src", "tgt"), "head"))
    return jax.shard_map(shards, mesh=mesh, in_specs=in_specs, out_specs=out_specs, check_vma=False)
```

```python
import functools

import jax
import jax.numpy as jnp
from jax import lax
from jax.experimental import pallas as pl
from jax.experimental.pallas import tpu as pltpu
from jax.sharding import PartitionSpec as P

DIM = 128
TILE = 128
SIDE = 4
TILES = SIDE * SIDE
WIDE = SIDE * TILE
ROWS = TILES * TILE
HALF = TILE // 2
PIECE = 32
QUERY = 0
GRAD = QUERY + HALF
DIGIT = GRAD + HALF
PACKED = DIGIT + 16
MASKED = -1e30
FLOOR = -1e29
SCALE = float(DIM) ** -0.5
LOG2E = 1.4426950408889634
LIMIT = 32 * 1024 * 1024


def dot(a, b, left, right):
    dims = (((left,), (right,)), ((), ()))
    return lax.dot_general(a, b, dims, preferred_element_type=jnp.float32)


def unit_rows(own, other, unit, low):
    parts = []
    for level in range(SIDE):
        for ref in (own, other):
            parts.append(ref[SIDE * level + unit, low : low + HALF, :])
    return jnp.concatenate(parts, axis=0)


def source_rows(kvs, level, low):
    parts = []
    for row in range(SIDE):
        for kv in kvs:
            parts.append(kv[SIDE * level + row, low : low + PIECE, :])
    return jnp.concatenate(parts, axis=0)


def source_steps(scalars, chunks):
    step = lax.broadcasted_iota(jnp.int32, (PIECE, WIDE), 0)
    return jnp.concatenate([step + scalars[SIDE + chunk] for chunk in chunks], axis=0)


def masked(block, steps, lim, level, row, lanes):
    size = steps.shape[0]
    part = block[row * size : (row + 1) * size]
    return jnp.where(steps < lim[SIDE * level + row, lanes][None, :], part, MASKED)


def unit_lanes(unit):
    return pl.ds(pl.multiple_of(unit * WIDE, WIDE), WIDE)


def stats_kernel(chunks, start, *refs):
    scalars, lim, own, other = refs[:4]
    kvs, refs = refs[4 : 4 + len(chunks)], refs[4 + len(chunks) :]
    out = refs[-1]
    if start:
        out[...] = jnp.zeros_like(out)
        out[0:1, :] = jnp.full((1, ROWS), MASKED, jnp.float32)
    else:
        out[...] = refs[0][...]
    size = PIECE * len(chunks)
    for level in range(SIDE):

        def unit_stats(unit, carry):
            lanes = unit_lanes(unit)
            steps = source_steps(scalars, chunks)
            x = unit_rows(own, other, unit, QUERY)
            g = unit_rows(own, other, unit, GRAD)
            product = dot(source_rows(kvs, level, 0), x, 1, 1)
            prods = dot(source_rows(kvs, level, PIECE), g, 1, 1)
            scores = [masked(product, steps, lim, level, row, lanes) for row in range(SIDE)]
            top = functools.reduce(jnp.maximum, scores).max(axis=0, keepdims=True)
            old = out[0:1, lanes]
            high = jnp.maximum(old, top * (SCALE * LOG2E))
            base = jnp.maximum(high, FLOOR)
            total = jnp.zeros((size, WIDE), jnp.float32)
            mixed = jnp.zeros((size, WIDE), jnp.float32)
            for row in range(SIDE):
                weights = jnp.exp2(scores[row] * (SCALE * LOG2E) - base)
                total += weights
                mixed += weights * prods[row * size : (row + 1) * size]
            fade = jnp.exp2(old - high)
            out[0:1, lanes] = high
            out[1:2, lanes] = out[1:2, lanes] * fade + total.sum(axis=0, keepdims=True)
            out[2:3, lanes] = out[2:3, lanes] * fade + mixed.sum(axis=0, keepdims=True)
            return carry

        lax.fori_loop(scalars[level], SIDE, unit_stats, 0)


def source_grads_kernel(scalars, lim, own, other, mine, theirs, kv0, kv1, kv2, kv3, *refs):
    kvs = (kv0, kv1, kv2, kv3)
    outs, (lows, shift, delta, key_acc, value_acc) = refs[:SIDE], refs[SIDE:]
    for tile in range(TILES):
        lanes = slice(tile * TILE, (tile + 1) * TILE)
        a = mine[:, lanes]
        b = pltpu.roll(theirs[:, lanes], HALF, 1)
        high = jnp.maximum(a[0:1], b[0:1])
        wa = jnp.exp2(a[0:1] - high)
        wb = jnp.exp2(b[0:1] - high)
        total = a[1:2] * wa + b[1:2] * wb
        mixed = a[2:3] * wa + b[2:3] * wb
        shift[0:1, lanes] = high + jnp.log2(total)
        delta[0:1, lanes] = mixed / total
    for level in range(SIDE):
        key_acc[...] = jnp.zeros_like(key_acc)
        value_acc[...] = jnp.zeros_like(value_acc)

        def unit_grads(unit, carry):
            lanes = unit_lanes(unit)
            steps = source_steps(scalars, range(SIDE))
            x = unit_rows(own, other, unit, QUERY)
            g = unit_rows(own, other, unit, GRAD)
            scores = dot(source_rows(kvs, level, 0), x, 1, 1) * (SCALE * LOG2E) - shift[0:1, lanes]
            prods = dot(source_rows(kvs, level, PIECE), g, 1, 1) - delta[0:1, lanes]
            highs = []
            parts = []
            for row in range(SIDE):
                probs = jnp.exp2(masked(scores, steps, lim, level, row, lanes))
                highs.append(probs.astype(jnp.bfloat16))
                parts.append((probs * prods[row * TILE : (row + 1) * TILE]).astype(jnp.bfloat16))
            low = jnp.concatenate(parts, axis=0)
            lows[SIDE * level + unit] = low
            value_acc[...] += dot(jnp.concatenate(highs, axis=0), g, 1, 0)
            key_acc[...] += dot(low, x, 1, 0)
            return carry

        lax.fori_loop(scalars[level], SIDE, unit_grads, 0)
        for row in range(SIDE):
            for index, out in enumerate(outs):
                begin = row * TILE + index * PIECE
                rows = slice(begin, begin + PIECE)
                tile = SIDE * level + row
                out[tile, 0:PIECE, :] = (key_acc[rows, :] * SCALE).astype(jnp.bfloat16)
                out[tile, PIECE : 2 * PIECE, :] = value_acc[rows, :].astype(jnp.bfloat16)


def query_grads_kernel(scalars, kv0, kv1, kv2, kv3, lows, keep, send, acc):
    kvs = (kv0, kv1, kv2, kv3)
    acc[...] = jnp.zeros_like(acc)
    for level in range(SIDE):

        def unit_grads(unit, carry):
            keys = source_rows(kvs, level, 0)
            acc[unit_lanes(unit), :] += dot(lows[SIDE * level + unit], keys, 0, 0)
            return carry

        lax.fori_loop(scalars[level], SIDE, unit_grads, 0)
    for unit in range(SIDE):
        for level in range(SIDE):
            begin = (SIDE * unit + level) * TILE
            tile = SIDE * level + unit
            keep[tile] = acc[begin : begin + HALF, :] * SCALE
            send[tile] = (acc[begin + HALF : begin + TILE, :] * SCALE).astype(jnp.bfloat16)


def pack_kernel(sums, keep, returned, out):
    out[:, : 2 * PIECE, :] = sums[...]
    out[:, 2 * PIECE :, :] = (keep[...] + returned[...].astype(jnp.float32)).astype(jnp.bfloat16)


SMEM = pl.BlockSpec(memory_space=pltpu.SMEM)
VMEM = pl.BlockSpec(memory_space=pltpu.VMEM)
PARAMS = pltpu.CompilerParams(vmem_limit_bytes=LIMIT)


def cost(chunks, dots):
    flops = 10 * len(chunks) * dots * 2 * PIECE * SIDE * WIDE * DIM
    return pl.CostEstimate(flops=flops, bytes_accessed=2**20, transcendentals=0)


def row_stats(chunks, scalars, lim, own, other, kvs, previous):
    operands = [scalars, lim, own, other] + [kvs[c] for c in chunks]
    if previous is not None:
        operands.append(previous)
    return pl.pallas_call(
        functools.partial(stats_kernel, chunks, previous is None),
        out_shape=jax.ShapeDtypeStruct((8, ROWS), jnp.float32),
        in_specs=[SMEM] + [VMEM] * (len(operands) - 1),
        out_specs=VMEM,
        compiler_params=PARAMS,
        cost_estimate=cost(chunks, 4),
        name="stats",
    )(*operands)


def source_grads(scalars, lim, own, other, mine, theirs, kvs):
    piece = jax.ShapeDtypeStruct((TILES, 2 * PIECE, DIM), jnp.bfloat16)
    lows = jax.ShapeDtypeStruct((TILES, WIDE, WIDE), jnp.bfloat16)
    operands = (scalars, lim, own, other, mine, theirs, *kvs)
    return pl.pallas_call(
        source_grads_kernel,
        out_shape=[piece] * SIDE + [lows],
        in_specs=[SMEM] + [VMEM] * (len(operands) - 1),
        out_specs=[VMEM] * (SIDE + 1),
        scratch_shapes=[
            pltpu.VMEM((8, ROWS), jnp.float32),
            pltpu.VMEM((8, ROWS), jnp.float32),
            pltpu.VMEM((WIDE, DIM), jnp.float32),
            pltpu.VMEM((WIDE, DIM), jnp.float32),
        ],
        compiler_params=PARAMS,
        cost_estimate=cost((0, 1, 2, 3), 4),
        name="source_grads",
    )(*operands)


def query_grads(scalars, kvs, lows):
    shape = (TILES, HALF, DIM)
    return pl.pallas_call(
        query_grads_kernel,
        out_shape=[jax.ShapeDtypeStruct(shape, jnp.float32), jax.ShapeDtypeStruct(shape, jnp.bfloat16)],
        in_specs=[SMEM] + [VMEM] * 5,
        out_specs=[VMEM] * 2,
        scratch_shapes=[pltpu.VMEM((ROWS, DIM), jnp.float32)],
        compiler_params=PARAMS,
        cost_estimate=cost((0, 1, 2, 3), 1),
        name="query_grads",
    )(scalars, *kvs, lows)


def pack_result(sums, keep, returned):
    return pl.pallas_call(
        pack_kernel,
        out_shape=jax.ShapeDtypeStruct((TILES, 2 * PIECE + HALF, DIM), jnp.bfloat16),
        in_specs=[VMEM] * 3,
        out_specs=VMEM,
        compiler_params=PARAMS,
        name="pack",
    )(sums, keep, returned)


def gather_kernel(*refs):
    out = refs[-1]
    for tile in range(TILES):
        low = 0
        for ref in refs[:-1]:
            high = low + ref.shape[0]
            wide = ref.shape[1] > DIM
            out[tile, low:high, :] = ref[:, tile * DIM : (tile + 1) * DIM] if wide else ref[...]
            low = high


def by_head(*arrays):
    rows = sum(a.shape[0] for a in arrays)
    return pl.pallas_call(
        gather_kernel,
        out_shape=jax.ShapeDtypeStruct((TILES, rows, DIM), jnp.bfloat16),
        in_specs=[VMEM] * len(arrays),
        out_specs=VMEM,
        compiler_params=PARAMS,
        name="by_head",
    )(*arrays)


def by_row_kernel(heads, keys, values, queries):
    for tile in range(TILES):
        columns = slice(tile * DIM, (tile + 1) * DIM)
        keys[:, columns] = heads[tile, :PIECE, :]
        values[:, columns] = heads[tile, PIECE : 2 * PIECE, :]
        queries[:, columns] = heads[tile, 2 * PIECE :, :]


def by_row(heads):
    rows = (PIECE, PIECE, HALF)
    return pl.pallas_call(
        by_row_kernel,
        out_shape=[jax.ShapeDtypeStruct((n, TILES * DIM), jnp.bfloat16) for n in rows],
        in_specs=[VMEM],
        out_specs=[VMEM] * 3,
        compiler_params=PARAMS,
        name="by_row",
    )(heads)


def device(row, column, level, core):
    return (row * SIDE + column) * 2 * SIDE + level * 2 + core


GROUPS = [
    [device(row, column, level, core) for level in range(SIDE) for row in range(SIDE)]
    for column in range(SIDE)
    for core in range(2)
]


def exchange(a):
    return lax.all_to_all(a, ("tgt", "src"), 0, 0, axis_index_groups=GROUPS, tiled=True)


def swap_cores(a):
    return lax.ppermute(a, "src", [(i, i ^ 1) for i in range(2 * SIDE)])


def along(a, shift):
    def target(i):
        return i - i % SIDE + (i + shift) % SIDE

    return lax.ppermute(a, "tgt", [(i, target(i)) for i in range(TILES)])


def shards(queries, keys, values, out_grad, read_points, block_mask):
    place = lax.axis_index("src")
    level, core = place // 2, place % 2
    column = lax.axis_index("tgt") % SIDE

    reads = lax.dynamic_slice_in_dim(read_points, level * TILE, TILE)
    digits = jnp.stack([reads // 64, reads % 64]).astype(jnp.bfloat16)
    digits = jnp.pad(digits, ((0, 14), (0, 0)))
    kv = exchange(by_head(keys, values))
    kvs = [kv] + [along(kv, k) for k in (1, 3, 2)]
    own = exchange(by_head(queries, out_grad, digits))
    other = swap_cores(own)

    reads = own[:, DIGIT].astype(jnp.int32) * 64 + own[:, DIGIT + 1].astype(jnp.int32)
    begins = (
        jnp.arange(SIDE, dtype=jnp.int32)[:, None] * (2 * WIDE)
        + core * WIDE
        + jnp.arange(SIDE, dtype=jnp.int32)[None, :] * TILE
    )
    tops = reads[TILES - SIDE :, -1]
    first = jnp.sum(tops[None, :] <= begins[:, :1], axis=1)
    offsets = jnp.stack([(column - k) % SIDE * PIECE for k in (0, 1, 3, 2)])
    scalars = jnp.concatenate([first, offsets]).astype(jnp.int32)
    ordered = jnp.where(core == 0, reads, jnp.roll(reads, HALF, axis=1))
    ordered = ordered.reshape(SIDE, SIDE, TILE).transpose(1, 0, 2)
    flags = block_mask.reshape(SIDE, SIDE, SIDE, SIDE, 2, SIDE)
    flags = lax.dynamic_index_in_dim(flags, column, 1, False)
    flags = lax.dynamic_index_in_dim(flags, core, 3, False).transpose(2, 3, 0, 1)
    lim = jnp.where(flags[..., None] == 1, ordered[None, None], 0) - begins[:, :, None, None, None]
    lim = lim.reshape(TILES, ROWS)

    common = (scalars, lim, own, other)
    mine = row_stats((0, 1, 2, 3), *common, kvs, None)
    theirs = swap_cores(mine)
    common += (mine, theirs, kvs)
    part0, part1, part2, part3, lows = source_grads(*common)
    got3, got1, got2 = along(part3, 2), along(part1, 3), along(part2, 1)
    keep, send = query_grads(scalars, kvs, lows)
    returned = swap_cores(send)
    sums = functools.reduce(jnp.add, [p.astype(jnp.float32) for p in (part0, got1, got2, got3)])
    result = pack_result(sums.astype(jnp.bfloat16), keep, returned)
    key_grad, value_grad, query_grad = by_row(exchange(result))
    return query_grad, key_grad, value_grad


def solution(mesh):
    in_specs = (
        P(("tgt", "src"), "head"),
        P(("src", "tgt"), "head"),
        P(("src", "tgt"), "head"),
        P(("tgt", "src"), "head"),
        P("tgt"),
        P(),
    )
    out_specs = (P(("tgt", "src"), "head"), P(("src", "tgt"), "head"), P(("src", "tgt"), "head"))
    return jax.shard_map(shards, mesh=mesh, in_specs=in_specs, out_specs=out_specs, check_vma=False)
```

```python
import functools

import jax
import jax.numpy as jnp
from jax import lax
from jax.experimental import pallas as pl
from jax.experimental.pallas import tpu as pltpu
from jax.sharding import PartitionSpec as P

DIM = 128
TILE = 128
SIDE = 4
TILES = SIDE * SIDE
WIDE = SIDE * TILE
ROWS = TILES * TILE
HALF = TILE // 2
PIECE = 32
QUERY = 0
GRAD = QUERY + HALF
DIGIT = GRAD + HALF
MASKED = -1e30
FLOOR = -1e29
SCALE = float(DIM) ** -0.5
LOG2E = 1.4426950408889634
LIMIT = 32 * 1024 * 1024


def dot(a, b, left, right):
    dims = (((left,), (right,)), ((), ()))
    return lax.dot_general(a, b, dims, preferred_element_type=jnp.float32)


def unit_rows(own, other, unit, low):
    parts = []
    for level in range(SIDE):
        for ref in (own, other):
            parts.append(ref[SIDE * level + unit, low : low + HALF, :])
    return jnp.concatenate(parts, axis=0)


def source_rows(kvs, level, low):
    parts = []
    for row in range(SIDE):
        for kv in kvs:
            parts.append(kv[SIDE * level + row, low : low + PIECE, :])
    return jnp.concatenate(parts, axis=0)


def source_steps(scalars):
    step = lax.broadcasted_iota(jnp.int32, (PIECE, WIDE), 0)
    return jnp.concatenate([step + scalars[SIDE + chunk] for chunk in range(SIDE)], axis=0)


def masked(block, steps, lim, level, row, lanes):
    part = block[row * TILE : (row + 1) * TILE]
    return jnp.where(steps < lim[SIDE * level + row, lanes][None, :], part, MASKED)


def unit_lanes(unit):
    return pl.ds(pl.multiple_of(unit * WIDE, WIDE), WIDE)


def stats_kernel(scalars, lim, own, other, kv0, kv1, kv2, kv3, out, acc):
    kvs = (kv0, kv1, kv2, kv3)
    acc[...] = jnp.zeros_like(acc)
    acc[0:8, :] = jnp.full((8, ROWS), MASKED, jnp.float32)
    for level in range(SIDE):

        def unit_stats(unit, carry):
            lanes = unit_lanes(unit)
            steps = source_steps(scalars)
            x = unit_rows(own, other, unit, QUERY)
            g = unit_rows(own, other, unit, GRAD)
            product = dot(source_rows(kvs, level, 0), x, 1, 1)
            prods = dot(source_rows(kvs, level, PIECE), g, 1, 1)
            high = acc[0:8, lanes]
            total = acc[8:16, lanes]
            mixed = acc[16:24, lanes]
            shape = (TILE // 8, 8, WIDE)
            for row in range(SIDE):
                block = masked(product, steps, lim, level, row, lanes).reshape(shape)
                part = prods[row * TILE : (row + 1) * TILE].reshape(shape)
                top = jnp.maximum(high, block.max(axis=0) * (SCALE * LOG2E))
                base = jnp.maximum(top, FLOOR)
                weights = jnp.exp2(block * (SCALE * LOG2E) - base[None])
                fade = jnp.exp2(high - top)
                total = total * fade + weights.sum(axis=0)
                mixed = mixed * fade + (weights * part).sum(axis=0)
                high = top
            acc[0:8, lanes] = high
            acc[8:16, lanes] = total
            acc[16:24, lanes] = mixed
            return carry

        lax.fori_loop(scalars[level], SIDE, unit_stats, 0)
    high = acc[0:8, :].max(axis=0, keepdims=True)
    fade = jnp.exp2(acc[0:8, :] - high)
    out[...] = jnp.zeros_like(out)
    out[0:1, :] = high
    out[1:2, :] = (acc[8:16, :] * fade).sum(axis=0, keepdims=True)
    out[2:3, :] = (acc[16:24, :] * fade).sum(axis=0, keepdims=True)


def source_grads_kernel(scalars, lim, own, other, mine, theirs, kv0, kv1, kv2, kv3, *refs):
    kvs = (kv0, kv1, kv2, kv3)
    outs, (lows, shift, delta, key_acc, value_acc) = refs[:SIDE], refs[SIDE:]
    for tile in range(TILES):
        lanes = slice(tile * TILE, (tile + 1) * TILE)
        a = mine[:, lanes]
        b = pltpu.roll(theirs[:, lanes], HALF, 1)
        high = jnp.maximum(a[0:1], b[0:1])
        wa = jnp.exp2(a[0:1] - high)
        wb = jnp.exp2(b[0:1] - high)
        total = a[1:2] * wa + b[1:2] * wb
        mixed = a[2:3] * wa + b[2:3] * wb
        shift[0:1, lanes] = high + jnp.log2(total)
        delta[0:1, lanes] = mixed / total
    for level in range(SIDE):
        key_acc[...] = jnp.zeros_like(key_acc)
        value_acc[...] = jnp.zeros_like(value_acc)

        def unit_grads(unit, carry):
            lanes = unit_lanes(unit)
            steps = source_steps(scalars)
            x = unit_rows(own, other, unit, QUERY)
            g = unit_rows(own, other, unit, GRAD)
            scores = dot(source_rows(kvs, level, 0), x, 1, 1) * (SCALE * LOG2E) - shift[0:1, lanes]
            prods = dot(source_rows(kvs, level, PIECE), g, 1, 1) - delta[0:1, lanes]
            highs = []
            parts = []
            for row in range(SIDE):
                probs = jnp.exp2(masked(scores, steps, lim, level, row, lanes))
                highs.append(probs.astype(jnp.bfloat16))
                parts.append((probs * prods[row * TILE : (row + 1) * TILE]).astype(jnp.bfloat16))
            low = jnp.concatenate(parts, axis=0)
            lows[SIDE * level + unit] = low
            value_acc[...] += dot(jnp.concatenate(highs, axis=0), g, 1, 0)
            key_acc[...] += dot(low, x, 1, 0)
            return carry

        lax.fori_loop(scalars[level], SIDE, unit_grads, 0)
        for row in range(SIDE):
            for index, out in enumerate(outs):
                begin = row * TILE + index * PIECE
                rows = slice(begin, begin + PIECE)
                tile = SIDE * level + row
                out[tile, 0:PIECE, :] = (key_acc[rows, :] * SCALE).astype(jnp.bfloat16)
                out[tile, PIECE : 2 * PIECE, :] = value_acc[rows, :].astype(jnp.bfloat16)


def query_grads_kernel(scalars, kv0, kv1, kv2, kv3, lows, keep, send, acc):
    kvs = (kv0, kv1, kv2, kv3)
    acc[...] = jnp.zeros_like(acc)
    for level in range(SIDE):

        def unit_grads(unit, carry):
            keys = source_rows(kvs, level, 0)
            acc[unit_lanes(unit), :] += dot(lows[SIDE * level + unit], keys, 0, 0)
            return carry

        lax.fori_loop(scalars[level], SIDE, unit_grads, 0)
    for unit in range(SIDE):
        for level in range(SIDE):
            begin = (SIDE * unit + level) * TILE
            tile = SIDE * level + unit
            keep[tile] = acc[begin : begin + HALF, :] * SCALE
            send[tile] = (acc[begin + HALF : begin + TILE, :] * SCALE).astype(jnp.bfloat16)


def pack_kernel(sums, keep, returned, out):
    out[:, : 2 * PIECE, :] = sums[...]
    out[:, 2 * PIECE :, :] = (keep[...] + returned[...].astype(jnp.float32)).astype(jnp.bfloat16)


SMEM = pl.BlockSpec(memory_space=pltpu.SMEM)
VMEM = pl.BlockSpec(memory_space=pltpu.VMEM)
PARAMS = pltpu.CompilerParams(vmem_limit_bytes=LIMIT)


def cost(dots):
    flops = 10 * dots * 2 * WIDE * WIDE * DIM
    return pl.CostEstimate(flops=flops, bytes_accessed=2**20, transcendentals=0)


def row_stats(scalars, lim, own, other, kvs):
    operands = (scalars, lim, own, other, *kvs)
    return pl.pallas_call(
        stats_kernel,
        out_shape=jax.ShapeDtypeStruct((8, ROWS), jnp.float32),
        in_specs=[SMEM] + [VMEM] * (len(operands) - 1),
        out_specs=VMEM,
        scratch_shapes=[pltpu.VMEM((24, ROWS), jnp.float32)],
        compiler_params=PARAMS,
        cost_estimate=cost(4),
        name="stats",
    )(*operands)


def source_grads(scalars, lim, own, other, mine, theirs, kvs):
    piece = jax.ShapeDtypeStruct((TILES, 2 * PIECE, DIM), jnp.bfloat16)
    lows = jax.ShapeDtypeStruct((TILES, WIDE, WIDE), jnp.bfloat16)
    operands = (scalars, lim, own, other, mine, theirs, *kvs)
    return pl.pallas_call(
        source_grads_kernel,
        out_shape=[piece] * SIDE + [lows],
        in_specs=[SMEM] + [VMEM] * (len(operands) - 1),
        out_specs=[VMEM] * (SIDE + 1),
        scratch_shapes=[
            pltpu.VMEM((8, ROWS), jnp.float32),
            pltpu.VMEM((8, ROWS), jnp.float32),
            pltpu.VMEM((WIDE, DIM), jnp.float32),
            pltpu.VMEM((WIDE, DIM), jnp.float32),
        ],
        compiler_params=PARAMS,
        cost_estimate=cost(4),
        name="source_grads",
    )(*operands)


def query_grads(scalars, kvs, lows):
    shape = (TILES, HALF, DIM)
    return pl.pallas_call(
        query_grads_kernel,
        out_shape=[jax.ShapeDtypeStruct(shape, jnp.float32), jax.ShapeDtypeStruct(shape, jnp.bfloat16)],
        in_specs=[SMEM] + [VMEM] * 5,
        out_specs=[VMEM] * 2,
        scratch_shapes=[pltpu.VMEM((ROWS, DIM), jnp.float32)],
        compiler_params=PARAMS,
        cost_estimate=cost(1),
        name="query_grads",
    )(scalars, *kvs, lows)


def pack_result(sums, keep, returned):
    return pl.pallas_call(
        pack_kernel,
        out_shape=jax.ShapeDtypeStruct((TILES, 2 * PIECE + HALF, DIM), jnp.bfloat16),
        in_specs=[VMEM] * 3,
        out_specs=VMEM,
        compiler_params=PARAMS,
        name="pack",
    )(sums, keep, returned)


def by_head_kernel(*refs):
    out = refs[-1]
    low = 0
    for ref in refs[:-1]:
        high = low + ref.shape[0]
        for tile in range(TILES):
            wide = ref.shape[1] > DIM
            out[tile, low:high, :] = ref[:, tile * DIM : (tile + 1) * DIM] if wide else ref[...]
        low = high


def by_head(*arrays):
    rows = sum(a.shape[0] for a in arrays)
    return pl.pallas_call(
        by_head_kernel,
        out_shape=jax.ShapeDtypeStruct((TILES, rows, DIM), jnp.bfloat16),
        in_specs=[VMEM] * len(arrays),
        out_specs=VMEM,
        name="by_head",
    )(*arrays)


def by_row_kernel(heads, keys, values, queries):
    for tile in range(TILES):
        columns = slice(tile * DIM, (tile + 1) * DIM)
        keys[:, columns] = heads[tile, :PIECE, :]
        values[:, columns] = heads[tile, PIECE : 2 * PIECE, :]
        queries[:, columns] = heads[tile, 2 * PIECE :, :]


def by_row(heads):
    rows = (PIECE, PIECE, HALF)
    return pl.pallas_call(
        by_row_kernel,
        out_shape=[jax.ShapeDtypeStruct((n, TILES * DIM), jnp.bfloat16) for n in rows],
        in_specs=[VMEM],
        out_specs=[VMEM] * 3,
        compiler_params=PARAMS,
        name="by_row",
    )(heads)


def device(row, column, level, core):
    return (row * SIDE + column) * 2 * SIDE + level * 2 + core


GROUPS = [
    [device(row, column, level, core) for level in range(SIDE) for row in range(SIDE)]
    for column in range(SIDE)
    for core in range(2)
]


def exchange(a):
    return lax.all_to_all(a, ("tgt", "src"), 0, 0, axis_index_groups=GROUPS, tiled=True)


def swap_cores(a):
    return lax.ppermute(a, "src", [(i, i ^ 1) for i in range(2 * SIDE)])


def along(a, shift):
    def target(i):
        return i - i % SIDE + (i + shift) % SIDE

    return lax.ppermute(a, "tgt", [(i, target(i)) for i in range(TILES)])


def shards(queries, keys, values, out_grad, read_points, block_mask):
    place = lax.axis_index("src")
    level, core = place // 2, place % 2
    column = lax.axis_index("tgt") % SIDE

    reads = lax.dynamic_slice_in_dim(read_points, level * TILE, TILE)
    digits = jnp.stack([reads // 64, reads % 64]).astype(jnp.bfloat16)
    digits = jnp.pad(digits, ((0, 14), (0, 0)))
    kv = exchange(by_head(keys, values))
    kvs = [kv] + [along(kv, k) for k in (1, 3, 2)]
    own = exchange(by_head(queries, out_grad, digits))
    other = swap_cores(own)

    reads = own[:, DIGIT].astype(jnp.int32) * 64 + own[:, DIGIT + 1].astype(jnp.int32)
    begins = (
        jnp.arange(SIDE, dtype=jnp.int32)[:, None] * (2 * WIDE)
        + core * WIDE
        + jnp.arange(SIDE, dtype=jnp.int32)[None, :] * TILE
    )
    tops = reads[TILES - SIDE :, -1]
    first = jnp.sum(tops[None, :] <= begins[:, :1], axis=1)
    offsets = jnp.stack([(column - k) % SIDE * PIECE for k in (0, 1, 3, 2)])
    scalars = jnp.concatenate([first, offsets]).astype(jnp.int32)
    ordered = jnp.where(core == 0, reads, jnp.roll(reads, HALF, axis=1))
    ordered = ordered.reshape(SIDE, SIDE, TILE).transpose(1, 0, 2)
    flags = block_mask.reshape(SIDE, SIDE, SIDE, SIDE, 2, SIDE)
    flags = lax.dynamic_index_in_dim(flags, column, 1, False)
    flags = lax.dynamic_index_in_dim(flags, core, 3, False).transpose(2, 3, 0, 1)
    lim = jnp.where(flags[..., None] == 1, ordered[None, None], 0) - begins[:, :, None, None, None]
    lim = lim.reshape(TILES, ROWS)

    common = (scalars, lim, own, other)
    mine = row_stats(*common, kvs)
    theirs = swap_cores(mine)
    common += (mine, theirs, kvs)
    part0, part1, part2, part3, lows = source_grads(*common)
    got3, got1, got2 = along(part3, 2), along(part1, 3), along(part2, 1)
    keep, send = query_grads(scalars, kvs, lows)
    returned = swap_cores(send)
    sums = functools.reduce(jnp.add, [p.astype(jnp.float32) for p in (part0, got1, got2, got3)])
    result = pack_result(sums.astype(jnp.bfloat16), keep, returned)
    key_grad, value_grad, query_grad = by_row(exchange(result))
    return query_grad, key_grad, value_grad


def solution(mesh):
    in_specs = (
        P(("tgt", "src"), "head"),
        P(("src", "tgt"), "head"),
        P(("src", "tgt"), "head"),
        P(("tgt", "src"), "head"),
        P("tgt"),
        P(),
    )
    out_specs = (P(("tgt", "src"), "head"), P(("src", "tgt"), "head"), P(("src", "tgt"), "head"))
    return jax.shard_map(shards, mesh=mesh, in_specs=in_specs, out_specs=out_specs, check_vma=False)
```

```python
import functools

import jax
import jax.numpy as jnp
from jax import lax
from jax.experimental import pallas as pl
from jax.experimental.pallas import tpu as pltpu
from jax.sharding import PartitionSpec as P

DIM = 128
TILE = 128
SIDE = 4
TILES = SIDE * SIDE
WIDE = SIDE * TILE
PART = WIDE // 2
ROWS = TILES * TILE
HALF = TILE // 2
PIECE = 32
QUERY = 0
GRAD = QUERY + HALF
DIGIT = GRAD + HALF
MASKED = -1e30
FLOOR = -1e29
SCALE = float(DIM) ** -0.5
LOG2E = 1.4426950408889634
LIMIT = 8 * 1024 * 1024


def dot(a, b, left, right):
    dims = (((left,), (right,)), ((), ()))
    return lax.dot_general(a, b, dims, preferred_element_type=jnp.float32)


def unit_rows(own, other, unit, low):
    parts = []
    for level in range(SIDE):
        for ref in (own, other):
            parts.append(ref[SIDE * level + unit, low : low + HALF, :])
    return jnp.concatenate(parts, axis=0)


def source_rows(kvs, level, low, count=SIDE):
    parts = []
    for row in range(count):
        for kv in kvs:
            parts.append(kv[SIDE * level + row, low : low + PIECE, :])
    return jnp.concatenate(parts, axis=0)


def source_steps(scalars):
    step = lax.broadcasted_iota(jnp.int32, (PIECE, WIDE), 0)
    return jnp.concatenate([step + scalars[SIDE + chunk] for chunk in range(SIDE)], axis=0)


def masked(block, steps, lim, level, row, lanes):
    part = block[row * TILE : (row + 1) * TILE]
    return jnp.where(steps < lim[SIDE * level + row, lanes][None, :], part, MASKED)


def unit_lanes(unit):
    return pl.ds(pl.multiple_of(unit * WIDE, WIDE), WIDE)


def for_units(scalars, level, body):
    first, whole = scalars[level], scalars[2 * SIDE + level]
    lax.fori_loop(first, whole, functools.partial(body, 1), 0)
    lax.fori_loop(whole, SIDE, functools.partial(body, SIDE), 0)


def stats_kernel(scalars, lim, own, other, kv0, kv1, kv2, kv3, out, logits, acc):
    kvs = (kv0, kv1, kv2, kv3)
    acc[...] = jnp.zeros_like(acc)
    acc[0:8, :] = jnp.full((8, ROWS), MASKED, jnp.float32)
    for level in range(SIDE):

        def unit_stats(count, unit, carry):
            lanes = unit_lanes(unit)
            steps = source_steps(scalars)
            x = unit_rows(own, other, unit, QUERY)
            g = unit_rows(own, other, unit, GRAD)
            product = dot(source_rows(kvs, level, 0, count), x, 1, 1)
            mixture = dot(source_rows(kvs, level, PIECE, count), g, 1, 1)
            high = acc[0:8, lanes]
            total = acc[8:16, lanes]
            mixed = acc[16:24, lanes]
            shape = (TILE // 8, 8, WIDE)
            for row in range(count):
                rows = slice(row * TILE, (row + 1) * TILE)
                block = masked(product, steps, lim, level, row, lanes) * (SCALE * LOG2E)
                logits[SIDE * level + unit, rows] = block
                top = jnp.maximum(high, block.reshape(shape).max(axis=0))
                base = jnp.maximum(top, FLOOR)
                weights = jnp.exp2(block.reshape(shape) - base[None])
                fade = jnp.exp2(high - top)
                total = total * fade + weights.sum(axis=0)
                mixed = mixed * fade + (weights * mixture[rows].reshape(shape)).sum(axis=0)
                high = top
            acc[0:8, lanes] = high
            acc[8:16, lanes] = total
            acc[16:24, lanes] = mixed
            return carry

        for_units(scalars, level, unit_stats)
    high = acc[0:8, :].max(axis=0, keepdims=True)
    fade = jnp.exp2(acc[0:8, :] - high)
    out[...] = jnp.zeros_like(out)
    out[0:1, :] = high
    out[1:2, :] = (acc[8:16, :] * fade).sum(axis=0, keepdims=True)
    out[2:3, :] = (acc[16:24, :] * fade).sum(axis=0, keepdims=True)


def source_grads_kernel(
    scalars, own, other, mine, theirs, logits, kv0, kv1, kv2, kv3, *refs
):
    kvs = (kv0, kv1, kv2, kv3)
    outs, (lows, shift, delta, key_acc, value_acc) = refs[:SIDE], refs[SIDE:]
    for tile in range(TILES):
        lanes = slice(tile * TILE, (tile + 1) * TILE)
        a = mine[:, lanes]
        b = pltpu.roll(theirs[:, lanes], HALF, 1)
        high = jnp.maximum(a[0:1], b[0:1])
        wa = jnp.exp2(a[0:1] - high)
        wb = jnp.exp2(b[0:1] - high)
        total = a[1:2] * wa + b[1:2] * wb
        mixed = a[2:3] * wa + b[2:3] * wb
        shift[0:1, lanes] = high + jnp.log2(total)
        delta[0:1, lanes] = mixed / total
    for level in range(SIDE):
        key_acc[...] = jnp.zeros_like(key_acc)
        value_acc[...] = jnp.zeros_like(value_acc)

        def unit_grads(count, unit, carry):
            x = unit_rows(own, other, unit, QUERY)
            g = unit_rows(own, other, unit, GRAD)
            values = source_rows(kvs, level, PIECE, count)
            key_sum = value_sum = 0.0
            for begin in range(0, WIDE, PART):
                lanes = pl.ds(pl.multiple_of(unit * WIDE + begin, PART), PART)
                x_part = x[begin : begin + PART]
                g_part = g[begin : begin + PART]
                columns = slice(begin, begin + PART)
                prods = dot(values, g_part, 1, 1) - delta[0:1, lanes]
                highs = []
                parts = []
                for row in range(count):
                    rows = slice(row * TILE, (row + 1) * TILE)
                    block = logits[SIDE * level + unit, rows, columns]
                    probs = jnp.exp2(block - shift[0:1, lanes])
                    highs.append(probs.astype(jnp.bfloat16))
                    parts.append((probs * prods[rows]).astype(jnp.bfloat16))
                low = jnp.concatenate(parts, axis=0)
                lows[SIDE * level + unit, : count * TILE, begin : begin + PART] = low
                value_sum += dot(jnp.concatenate(highs, axis=0), g_part, 1, 0)
                key_sum += dot(low, x_part, 1, 0)
            key_acc[: count * TILE] += key_sum
            value_acc[: count * TILE] += value_sum
            return carry

        for_units(scalars, level, unit_grads)
        for row in range(SIDE):
            for index, out in enumerate(outs):
                begin = row * TILE + index * PIECE
                rows = slice(begin, begin + PIECE)
                tile = SIDE * level + row
                out[tile, 0:PIECE, :] = (key_acc[rows, :] * SCALE).astype(jnp.bfloat16)
                out[tile, PIECE : 2 * PIECE, :] = value_acc[rows, :].astype(jnp.bfloat16)


def query_grads_kernel(scalars, kv0, kv1, kv2, kv3, lows, keep, send, acc):
    kvs = (kv0, kv1, kv2, kv3)
    acc[...] = jnp.zeros_like(acc)
    for level in range(SIDE):

        def unit_grads(count, unit, carry):
            low = lows[SIDE * level + unit, : count * TILE]
            acc[unit_lanes(unit), :] += dot(low, source_rows(kvs, level, 0, count), 0, 0)
            return carry

        for_units(scalars, level, unit_grads)
    for unit in range(SIDE):
        for level in range(SIDE):
            begin = (SIDE * unit + level) * TILE
            tile = SIDE * level + unit
            keep[tile] = acc[begin : begin + HALF, :] * SCALE
            send[tile] = (acc[begin + HALF : begin + TILE, :] * SCALE).astype(jnp.bfloat16)


def pack_kernel(sums, keep, returned, out):
    out[:, : 2 * PIECE, :] = sums[...]
    out[:, 2 * PIECE :, :] = (keep[...] + returned[...].astype(jnp.float32)).astype(jnp.bfloat16)


SMEM = pl.BlockSpec(memory_space=pltpu.SMEM)
VMEM = pl.BlockSpec(memory_space=pltpu.VMEM)
PARAMS = pltpu.CompilerParams(vmem_limit_bytes=LIMIT)


def cost(dots):
    flops = 10 * dots * 2 * WIDE * WIDE * DIM
    return pl.CostEstimate(flops=flops, bytes_accessed=2**20, transcendentals=0)


def row_stats(scalars, lim, own, other, kvs):
    operands = (scalars, lim, own, other, *kvs)
    return pl.pallas_call(
        stats_kernel,
        out_shape=[jax.ShapeDtypeStruct((8, ROWS), jnp.float32)]
        + [jax.ShapeDtypeStruct((TILES, WIDE, WIDE), jnp.float32)],
        in_specs=[SMEM] + [VMEM] * (len(operands) - 1),
        out_specs=[VMEM] * 2,
        scratch_shapes=[pltpu.VMEM((24, ROWS), jnp.float32)],
        compiler_params=PARAMS,
        cost_estimate=cost(4),
        name="stats",
    )(*operands)


def source_grads(*operands):
    piece = jax.ShapeDtypeStruct((TILES, 2 * PIECE, DIM), jnp.bfloat16)
    lows = jax.ShapeDtypeStruct((TILES, WIDE, WIDE), jnp.bfloat16)
    return pl.pallas_call(
        source_grads_kernel,
        out_shape=[piece] * SIDE + [lows],
        in_specs=[SMEM] + [VMEM] * (len(operands) - 1),
        out_specs=[VMEM] * (SIDE + 1),
        scratch_shapes=[
            pltpu.VMEM((8, ROWS), jnp.float32),
            pltpu.VMEM((8, ROWS), jnp.float32),
            pltpu.VMEM((WIDE, DIM), jnp.float32),
            pltpu.VMEM((WIDE, DIM), jnp.float32),
        ],
        compiler_params=PARAMS,
        cost_estimate=cost(4),
        name="source_grads",
    )(*operands)


def query_grads(scalars, kvs, lows):
    shape = (TILES, HALF, DIM)
    return pl.pallas_call(
        query_grads_kernel,
        out_shape=[jax.ShapeDtypeStruct(shape, jnp.float32), jax.ShapeDtypeStruct(shape, jnp.bfloat16)],
        in_specs=[SMEM] + [VMEM] * 5,
        out_specs=[VMEM] * 2,
        scratch_shapes=[pltpu.VMEM((ROWS, DIM), jnp.float32)],
        compiler_params=PARAMS,
        cost_estimate=cost(1),
        name="query_grads",
    )(scalars, *kvs, lows)


def pack_result(sums, keep, returned):
    return pl.pallas_call(
        pack_kernel,
        out_shape=jax.ShapeDtypeStruct((TILES, 2 * PIECE + HALF, DIM), jnp.bfloat16),
        in_specs=[VMEM] * 3,
        out_specs=VMEM,
        compiler_params=PARAMS,
        name="pack",
    )(sums, keep, returned)


def by_head_kernel(*refs):
    out = refs[-1]
    low = 0
    for ref in refs[:-1]:
        high = low + ref.shape[0]
        for tile in range(TILES):
            wide = ref.shape[1] > DIM
            out[tile, low:high, :] = ref[:, tile * DIM : (tile + 1) * DIM] if wide else ref[...]
        low = high


def by_head(*arrays):
    rows = sum(a.shape[0] for a in arrays)
    return pl.pallas_call(
        by_head_kernel,
        out_shape=jax.ShapeDtypeStruct((TILES, rows, DIM), jnp.bfloat16),
        in_specs=[VMEM] * len(arrays),
        out_specs=VMEM,
        name="by_head",
    )(*arrays)


def by_row_kernel(heads, keys, values, queries):
    for tile in range(TILES):
        columns = slice(tile * DIM, (tile + 1) * DIM)
        keys[:, columns] = heads[tile, :PIECE, :]
        values[:, columns] = heads[tile, PIECE : 2 * PIECE, :]
        queries[:, columns] = heads[tile, 2 * PIECE :, :]


def by_row(heads):
    rows = (PIECE, PIECE, HALF)
    return pl.pallas_call(
        by_row_kernel,
        out_shape=[jax.ShapeDtypeStruct((n, TILES * DIM), jnp.bfloat16) for n in rows],
        in_specs=[VMEM],
        out_specs=[VMEM] * 3,
        compiler_params=PARAMS,
        name="by_row",
    )(heads)


def device(row, column, level, core):
    return (row * SIDE + column) * 2 * SIDE + level * 2 + core


GROUPS = [
    [device(row, column, level, core) for level in range(SIDE) for row in range(SIDE)]
    for column in range(SIDE)
    for core in range(2)
]


def exchange(a):
    return lax.all_to_all(a, ("tgt", "src"), 0, 0, axis_index_groups=GROUPS, tiled=True)


def swap_cores(a):
    return lax.ppermute(a, "src", [(i, i ^ 1) for i in range(2 * SIDE)])


def along(a, shift):
    def target(i):
        return i - i % SIDE + (i + shift) % SIDE

    return lax.ppermute(a, "tgt", [(i, target(i)) for i in range(TILES)])


def shards(queries, keys, values, out_grad, read_points, block_mask):
    place = lax.axis_index("src")
    level, core = place // 2, place % 2
    column = lax.axis_index("tgt") % SIDE

    reads = lax.dynamic_slice_in_dim(read_points, level * TILE, TILE)
    digits = jnp.stack([reads // 64, reads % 64]).astype(jnp.bfloat16)
    digits = jnp.pad(digits, ((0, 14), (0, 0)))
    kv = exchange(by_head(keys, values))
    kvs = [kv] + [along(kv, k) for k in (1, 3, 2)]
    own = exchange(by_head(queries, out_grad, digits))
    other = swap_cores(own)

    reads = own[:, DIGIT].astype(jnp.int32) * 64 + own[:, DIGIT + 1].astype(jnp.int32)
    begins = (
        jnp.arange(SIDE, dtype=jnp.int32)[:, None] * (2 * WIDE)
        + core * WIDE
        + jnp.arange(SIDE, dtype=jnp.int32)[None, :] * TILE
    )
    tops = reads[TILES - SIDE :, -1]
    first = jnp.sum(tops[None, :] <= begins[:, :1], axis=1)
    whole = jnp.sum(tops[None, :] <= begins[:, 1:2], axis=1)
    offsets = jnp.stack([(column - k) % SIDE * PIECE for k in (0, 1, 3, 2)])
    scalars = jnp.concatenate([first, offsets, whole]).astype(jnp.int32)
    ordered = jnp.where(core == 0, reads, jnp.roll(reads, HALF, axis=1))
    ordered = ordered.reshape(SIDE, SIDE, TILE).transpose(1, 0, 2)
    flags = block_mask.reshape(SIDE, SIDE, SIDE, SIDE, 2, SIDE)
    flags = lax.dynamic_index_in_dim(flags, column, 1, False)
    flags = lax.dynamic_index_in_dim(flags, core, 3, False).transpose(2, 3, 0, 1)
    lim = jnp.where(flags[..., None] == 1, ordered[None, None], 0) - begins[:, :, None, None, None]
    lim = lim.reshape(TILES, ROWS)

    mine, logits = row_stats(scalars, lim, own, other, kvs)
    theirs = swap_cores(mine)
    part0, part1, part2, part3, lows = source_grads(
        scalars, own, other, mine, theirs, logits, *kvs
    )
    got3, got1, got2 = along(part3, 2), along(part1, 3), along(part2, 1)
    keep, send = query_grads(scalars, kvs, lows)
    returned = swap_cores(send)
    sums = functools.reduce(jnp.add, [p.astype(jnp.float32) for p in (part0, got1, got2, got3)])
    result = pack_result(sums.astype(jnp.bfloat16), keep, returned)
    key_grad, value_grad, query_grad = by_row(exchange(result))
    return query_grad, key_grad, value_grad


def solution(mesh):
    in_specs = (
        P(("tgt", "src"), "head"),
        P(("src", "tgt"), "head"),
        P(("src", "tgt"), "head"),
        P(("tgt", "src"), "head"),
        P("tgt"),
        P(),
    )
    out_specs = (P(("tgt", "src"), "head"), P(("src", "tgt"), "head"), P(("src", "tgt"), "head"))
    return jax.shard_map(shards, mesh=mesh, in_specs=in_specs, out_specs=out_specs, check_vma=False)
```

```python
import functools

import jax
import jax.numpy as jnp
from jax import lax
from jax.experimental import pallas as pl
from jax.experimental.pallas import tpu as pltpu
from jax.sharding import PartitionSpec as P

DIM = 128
TILE = 128
SIDE = 4
TILES = SIDE * SIDE
WIDE = SIDE * TILE
PART = WIDE // 2
ROWS = TILES * TILE
HALF = TILE // 2
PIECE = 32
QUERY = 0
GRAD = QUERY + HALF
DIGIT = GRAD + HALF
MASKED = -1e30
FLOOR = -1e29
SCALE = float(DIM) ** -0.5
LOG2E = 1.4426950408889634
LIMIT = 4 * 1024 * 1024


def dot(a, b, left, right):
    dims = (((left,), (right,)), ((), ()))
    return lax.dot_general(a, b, dims, preferred_element_type=jnp.float32)


def unit_rows(own, other, unit, low):
    parts = []
    for level in range(SIDE):
        for ref in (own, other):
            parts.append(ref[SIDE * level + unit, low : low + HALF, :])
    return jnp.concatenate(parts, axis=0)


def source_rows(kvs, level, low, count=SIDE):
    parts = []
    for row in range(count):
        for kv in kvs:
            parts.append(kv[SIDE * level + row, low : low + PIECE, :])
    return jnp.concatenate(parts, axis=0)


def source_steps(scalars):
    step = lax.broadcasted_iota(jnp.int32, (PIECE, WIDE), 0)
    return jnp.concatenate([step + scalars[SIDE + chunk] for chunk in range(SIDE)], axis=0)


def masked(block, steps, lim, level, row, lanes):
    part = block[row * TILE : (row + 1) * TILE]
    return jnp.where(steps < lim[SIDE * level + row, lanes][None, :], part, MASKED)


def unit_lanes(unit):
    return pl.ds(pl.multiple_of(unit * WIDE, WIDE), WIDE)


def for_units(scalars, level, body):
    first, whole = scalars[level], scalars[2 * SIDE + level]
    lax.fori_loop(first, whole, functools.partial(body, 1), 0)
    lax.fori_loop(whole, SIDE, functools.partial(body, SIDE), 0)


def stats_kernel(scalars, lim, own, other, kv0, kv1, kv2, kv3, out, logits, prods, acc):
    kvs = (kv0, kv1, kv2, kv3)
    acc[...] = jnp.zeros_like(acc)
    acc[0:8, :] = jnp.full((8, ROWS), MASKED, jnp.float32)
    for level in range(SIDE):

        def unit_stats(count, unit, carry):
            lanes = unit_lanes(unit)
            steps = source_steps(scalars)
            x = unit_rows(own, other, unit, QUERY)
            g = unit_rows(own, other, unit, GRAD)
            product = dot(source_rows(kvs, level, 0, count), x, 1, 1)
            mixture = dot(source_rows(kvs, level, PIECE, count), g, 1, 1)
            high = acc[0:8, lanes]
            total = acc[8:16, lanes]
            mixed = acc[16:24, lanes]
            shape = (TILE // 8, 8, WIDE)
            for row in range(count):
                rows = slice(row * TILE, (row + 1) * TILE)
                block = masked(product, steps, lim, level, row, lanes) * (SCALE * LOG2E)
                logits[SIDE * level + unit, rows] = block
                prods[SIDE * level + unit, rows] = mixture[rows]
                top = jnp.maximum(high, block.reshape(shape).max(axis=0))
                base = jnp.maximum(top, FLOOR)
                weights = jnp.exp2(block.reshape(shape) - base[None])
                fade = jnp.exp2(high - top)
                total = total * fade + weights.sum(axis=0)
                mixed = mixed * fade + (weights * mixture[rows].reshape(shape)).sum(axis=0)
                high = top
            acc[0:8, lanes] = high
            acc[8:16, lanes] = total
            acc[16:24, lanes] = mixed
            return carry

        for_units(scalars, level, unit_stats)
    high = acc[0:8, :].max(axis=0, keepdims=True)
    fade = jnp.exp2(acc[0:8, :] - high)
    out[...] = jnp.zeros_like(out)
    out[0:1, :] = high
    out[1:2, :] = (acc[8:16, :] * fade).sum(axis=0, keepdims=True)
    out[2:3, :] = (acc[16:24, :] * fade).sum(axis=0, keepdims=True)


def source_grads_kernel(scalars, own, other, mine, theirs, logits, prods, *refs):
    outs, (lows, shift, delta, key_acc, value_acc) = refs[:SIDE], refs[SIDE:]
    for tile in range(TILES):
        lanes = slice(tile * TILE, (tile + 1) * TILE)
        a = mine[:, lanes]
        b = pltpu.roll(theirs[:, lanes], HALF, 1)
        high = jnp.maximum(a[0:1], b[0:1])
        wa = jnp.exp2(a[0:1] - high)
        wb = jnp.exp2(b[0:1] - high)
        total = a[1:2] * wa + b[1:2] * wb
        mixed = a[2:3] * wa + b[2:3] * wb
        shift[0:1, lanes] = high + jnp.log2(total)
        delta[0:1, lanes] = mixed / total
    for level in range(SIDE):
        key_acc[...] = jnp.zeros_like(key_acc)
        value_acc[...] = jnp.zeros_like(value_acc)

        def unit_grads(count, unit, carry):
            x = unit_rows(own, other, unit, QUERY)
            g = unit_rows(own, other, unit, GRAD)
            key_sum = value_sum = 0.0
            for begin in range(0, WIDE, PART):
                lanes = pl.ds(pl.multiple_of(unit * WIDE + begin, PART), PART)
                x_part = x[begin : begin + PART]
                g_part = g[begin : begin + PART]
                columns = slice(begin, begin + PART)
                highs = []
                parts = []
                for row in range(count):
                    place = (SIDE * level + unit, slice(row * TILE, (row + 1) * TILE), columns)
                    probs = jnp.exp2(logits[place] - shift[0:1, lanes])
                    highs.append(probs.astype(jnp.bfloat16))
                    parts.append((probs * (prods[place] - delta[0:1, lanes])).astype(jnp.bfloat16))
                low = jnp.concatenate(parts, axis=0)
                lows[SIDE * level + unit, : count * TILE, begin : begin + PART] = low
                value_sum += dot(jnp.concatenate(highs, axis=0), g_part, 1, 0)
                key_sum += dot(low, x_part, 1, 0)
            key_acc[: count * TILE] += key_sum
            value_acc[: count * TILE] += value_sum
            return carry

        for_units(scalars, level, unit_grads)
        for row in range(SIDE):
            for index, out in enumerate(outs):
                begin = row * TILE + index * PIECE
                rows = slice(begin, begin + PIECE)
                tile = SIDE * level + row
                out[tile, 0:PIECE, :] = (key_acc[rows, :] * SCALE).astype(jnp.bfloat16)
                out[tile, PIECE : 2 * PIECE, :] = value_acc[rows, :].astype(jnp.bfloat16)


def query_grads_kernel(scalars, kv0, kv1, kv2, kv3, lows, keep, send, acc):
    kvs = (kv0, kv1, kv2, kv3)
    acc[...] = jnp.zeros_like(acc)
    for level in range(SIDE):

        def unit_grads(count, unit, carry):
            low = lows[SIDE * level + unit, : count * TILE]
            acc[unit_lanes(unit), :] += dot(low, source_rows(kvs, level, 0, count), 0, 0)
            return carry

        for_units(scalars, level, unit_grads)
    for unit in range(SIDE):
        for level in range(SIDE):
            begin = (SIDE * unit + level) * TILE
            tile = SIDE * level + unit
            keep[tile] = acc[begin : begin + HALF, :] * SCALE
            send[tile] = (acc[begin + HALF : begin + TILE, :] * SCALE).astype(jnp.bfloat16)


def pack_kernel(sums, keep, returned, out):
    out[:, : 2 * PIECE, :] = sums[...]
    out[:, 2 * PIECE :, :] = (keep[...] + returned[...].astype(jnp.float32)).astype(jnp.bfloat16)


SMEM = pl.BlockSpec(memory_space=pltpu.SMEM)
VMEM = pl.BlockSpec(memory_space=pltpu.VMEM)
PARAMS = pltpu.CompilerParams(vmem_limit_bytes=LIMIT)


def cost(dots):
    flops = 10 * dots * 2 * WIDE * WIDE * DIM
    return pl.CostEstimate(flops=flops, bytes_accessed=2**20, transcendentals=0)


def row_stats(scalars, lim, own, other, kvs):
    operands = (scalars, lim, own, other, *kvs)
    return pl.pallas_call(
        stats_kernel,
        out_shape=[jax.ShapeDtypeStruct((8, ROWS), jnp.float32)]
        + [jax.ShapeDtypeStruct((TILES, WIDE, WIDE), jnp.float32)] * 2,
        in_specs=[SMEM] + [VMEM] * (len(operands) - 1),
        out_specs=[VMEM] * 3,
        scratch_shapes=[pltpu.VMEM((24, ROWS), jnp.float32)],
        compiler_params=PARAMS,
        cost_estimate=cost(4),
        name="stats",
    )(*operands)


def source_grads(*operands):
    piece = jax.ShapeDtypeStruct((TILES, 2 * PIECE, DIM), jnp.bfloat16)
    lows = jax.ShapeDtypeStruct((TILES, WIDE, WIDE), jnp.bfloat16)
    return pl.pallas_call(
        source_grads_kernel,
        out_shape=[piece] * SIDE + [lows],
        in_specs=[SMEM] + [VMEM] * (len(operands) - 1),
        out_specs=[VMEM] * (SIDE + 1),
        scratch_shapes=[
            pltpu.VMEM((8, ROWS), jnp.float32),
            pltpu.VMEM((8, ROWS), jnp.float32),
            pltpu.VMEM((WIDE, DIM), jnp.float32),
            pltpu.VMEM((WIDE, DIM), jnp.float32),
        ],
        compiler_params=PARAMS,
        cost_estimate=cost(4),
        name="source_grads",
    )(*operands)


def query_grads(scalars, kvs, lows):
    shape = (TILES, HALF, DIM)
    return pl.pallas_call(
        query_grads_kernel,
        out_shape=[jax.ShapeDtypeStruct(shape, jnp.float32), jax.ShapeDtypeStruct(shape, jnp.bfloat16)],
        in_specs=[SMEM] + [VMEM] * 5,
        out_specs=[VMEM] * 2,
        scratch_shapes=[pltpu.VMEM((ROWS, DIM), jnp.float32)],
        compiler_params=PARAMS,
        cost_estimate=cost(1),
        name="query_grads",
    )(scalars, *kvs, lows)


def pack_result(sums, keep, returned):
    return pl.pallas_call(
        pack_kernel,
        out_shape=jax.ShapeDtypeStruct((TILES, 2 * PIECE + HALF, DIM), jnp.bfloat16),
        in_specs=[VMEM] * 3,
        out_specs=VMEM,
        compiler_params=PARAMS,
        name="pack",
    )(sums, keep, returned)


def by_head_kernel(*refs):
    out = refs[-1]
    low = 0
    for ref in refs[:-1]:
        high = low + ref.shape[0]
        for tile in range(TILES):
            wide = ref.shape[1] > DIM
            out[tile, low:high, :] = ref[:, tile * DIM : (tile + 1) * DIM] if wide else ref[...]
        low = high


def by_head(*arrays):
    rows = sum(a.shape[0] for a in arrays)
    return pl.pallas_call(
        by_head_kernel,
        out_shape=jax.ShapeDtypeStruct((TILES, rows, DIM), jnp.bfloat16),
        in_specs=[VMEM] * len(arrays),
        out_specs=VMEM,
        name="by_head",
    )(*arrays)


def by_row_kernel(heads, keys, values, queries):
    for tile in range(TILES):
        columns = slice(tile * DIM, (tile + 1) * DIM)
        keys[:, columns] = heads[tile, :PIECE, :]
        values[:, columns] = heads[tile, PIECE : 2 * PIECE, :]
        queries[:, columns] = heads[tile, 2 * PIECE :, :]


def by_row(heads):
    rows = (PIECE, PIECE, HALF)
    return pl.pallas_call(
        by_row_kernel,
        out_shape=[jax.ShapeDtypeStruct((n, TILES * DIM), jnp.bfloat16) for n in rows],
        in_specs=[VMEM],
        out_specs=[VMEM] * 3,
        compiler_params=PARAMS,
        name="by_row",
    )(heads)


def device(row, column, level, core):
    return (row * SIDE + column) * 2 * SIDE + level * 2 + core


GROUPS = [
    [device(row, column, level, core) for level in range(SIDE) for row in range(SIDE)]
    for column in range(SIDE)
    for core in range(2)
]


def exchange(a):
    return lax.all_to_all(a, ("tgt", "src"), 0, 0, axis_index_groups=GROUPS, tiled=True)


def swap_cores(a):
    return lax.ppermute(a, "src", [(i, i ^ 1) for i in range(2 * SIDE)])


def along(a, shift):
    def target(i):
        return i - i % SIDE + (i + shift) % SIDE

    return lax.ppermute(a, "tgt", [(i, target(i)) for i in range(TILES)])


def shards(queries, keys, values, out_grad, read_points, block_mask):
    place = lax.axis_index("src")
    level, core = place // 2, place % 2
    column = lax.axis_index("tgt") % SIDE

    reads = lax.dynamic_slice_in_dim(read_points, level * TILE, TILE)
    digits = jnp.stack([reads // 64, reads % 64]).astype(jnp.bfloat16)
    digits = jnp.pad(digits, ((0, 14), (0, 0)))
    kv = exchange(by_head(keys, values))
    kvs = [kv] + [along(kv, k) for k in (1, 3, 2)]
    own = exchange(by_head(queries, out_grad, digits))
    other = swap_cores(own)

    reads = own[:, DIGIT].astype(jnp.int32) * 64 + own[:, DIGIT + 1].astype(jnp.int32)
    begins = (
        jnp.arange(SIDE, dtype=jnp.int32)[:, None] * (2 * WIDE)
        + core * WIDE
        + jnp.arange(SIDE, dtype=jnp.int32)[None, :] * TILE
    )
    tops = reads[TILES - SIDE :, -1]
    first = jnp.sum(tops[None, :] <= begins[:, :1], axis=1)
    whole = jnp.sum(tops[None, :] <= begins[:, 1:2], axis=1)
    offsets = jnp.stack([(column - k) % SIDE * PIECE for k in (0, 1, 3, 2)])
    scalars = jnp.concatenate([first, offsets, whole]).astype(jnp.int32)
    ordered = jnp.where(core == 0, reads, jnp.roll(reads, HALF, axis=1))
    ordered = ordered.reshape(SIDE, SIDE, TILE).transpose(1, 0, 2)
    flags = block_mask.reshape(SIDE, SIDE, SIDE, SIDE, 2, SIDE)
    flags = lax.dynamic_index_in_dim(flags, column, 1, False)
    flags = lax.dynamic_index_in_dim(flags, core, 3, False).transpose(2, 3, 0, 1)
    lim = jnp.where(flags[..., None] == 1, ordered[None, None], 0) - begins[:, :, None, None, None]
    lim = lim.reshape(TILES, ROWS)

    mine, logits, prods = row_stats(scalars, lim, own, other, kvs)
    theirs = swap_cores(mine)
    part0, part1, part2, part3, lows = source_grads(
        scalars, own, other, mine, theirs, logits, prods
    )
    got3, got1, got2 = along(part3, 2), along(part1, 3), along(part2, 1)
    keep, send = query_grads(scalars, kvs, lows)
    returned = swap_cores(send)
    sums = functools.reduce(jnp.add, [p.astype(jnp.float32) for p in (part0, got1, got2, got3)])
    result = pack_result(sums.astype(jnp.bfloat16), keep, returned)
    key_grad, value_grad, query_grad = by_row(exchange(result))
    return query_grad, key_grad, value_grad


def solution(mesh):
    in_specs = (
        P(("tgt", "src"), "head"),
        P(("src", "tgt"), "head"),
        P(("src", "tgt"), "head"),
        P(("tgt", "src"), "head"),
        P("tgt"),
        P(),
    )
    out_specs = (P(("tgt", "src"), "head"), P(("src", "tgt"), "head"), P(("src", "tgt"), "head"))
    return jax.shard_map(shards, mesh=mesh, in_specs=in_specs, out_specs=out_specs, check_vma=False)
```

```python
import functools

import jax
import jax.numpy as jnp
from jax import lax
from jax.experimental import pallas as pl
from jax.experimental.pallas import tpu as pltpu
from jax.sharding import PartitionSpec as P

DIM = 128
TILE = 128
SIDE = 4
TILES = SIDE * SIDE
WIDE = SIDE * TILE
PART = WIDE // 2
ROWS = TILES * TILE
HALF = TILE // 2
PIECE = 32
QUERY = 0
GRAD = QUERY + HALF
DIGIT = GRAD + HALF
MASKED = -1e30
FLOOR = -1e29
SCALE = float(DIM) ** -0.5
LOG2E = 1.4426950408889634
LIMIT = 4 * 1024 * 1024


def dot(a, b, left, right):
    dims = (((left,), (right,)), ((), ()))
    return lax.dot_general(a, b, dims, preferred_element_type=jnp.float32)


def unit_rows(own, other, unit, low):
    parts = []
    for level in range(SIDE):
        for ref in (own, other):
            parts.append(ref[SIDE * level + unit, low : low + HALF, :])
    return jnp.concatenate(parts, axis=0)


def source_rows(kvs, level, low, count=SIDE):
    parts = []
    for row in range(count):
        for kv in kvs:
            parts.append(kv[SIDE * level + row, low : low + PIECE, :])
    return jnp.concatenate(parts, axis=0)


def source_steps(scalars):
    step = lax.broadcasted_iota(jnp.int32, (PIECE, WIDE), 0)
    return jnp.concatenate([step + scalars[SIDE + chunk] for chunk in range(SIDE)], axis=0)


def masked(block, steps, lim, level, row, lanes):
    part = block[row * TILE : (row + 1) * TILE]
    return jnp.where(steps < lim[SIDE * level + row, lanes][None, :], part, MASKED)


def unit_lanes(unit):
    return pl.ds(pl.multiple_of(unit * WIDE, WIDE), WIDE)


def for_units(scalars, level, body):
    first, whole = scalars[level], scalars[2 * SIDE + level]
    lax.fori_loop(first, whole, functools.partial(body, 1), 0)
    lax.fori_loop(whole, SIDE, functools.partial(body, SIDE), 0)


def stats_kernel(scalars, lim, own, other, kv0, kv1, kv2, kv3, out, logits, prods, acc):
    kvs = (kv0, kv1, kv2, kv3)
    acc[...] = jnp.zeros_like(acc)
    acc[0:8, :] = jnp.full((8, ROWS), MASKED, jnp.float32)
    for level in range(SIDE):

        def unit_stats(count, unit, carry):
            lanes = unit_lanes(unit)
            steps = source_steps(scalars)
            x = unit_rows(own, other, unit, QUERY)
            g = unit_rows(own, other, unit, GRAD)
            product = dot(source_rows(kvs, level, 0, count), x, 1, 1)
            mixture = dot(source_rows(kvs, level, PIECE, count), g, 1, 1)
            high = acc[0:8, lanes]
            total = acc[8:16, lanes]
            mixed = acc[16:24, lanes]
            shape = (TILE // 8, 8, WIDE)
            for row in range(count):
                rows = slice(row * TILE, (row + 1) * TILE)
                block = masked(product, steps, lim, level, row, lanes) * (SCALE * LOG2E)
                logits[SIDE * level + unit, rows] = block
                prods[SIDE * level + unit, rows] = mixture[rows]
                top = jnp.maximum(high, block.reshape(shape).max(axis=0))
                base = jnp.maximum(top, FLOOR)
                weights = jnp.exp2(block.reshape(shape) - base[None])
                fade = jnp.exp2(high - top)
                total = total * fade + weights.sum(axis=0)
                mixed = mixed * fade + (weights * mixture[rows].reshape(shape)).sum(axis=0)
                high = top
            acc[0:8, lanes] = high
            acc[8:16, lanes] = total
            acc[16:24, lanes] = mixed
            return carry

        for_units(scalars, level, unit_stats)
    high = acc[0:8, :].max(axis=0, keepdims=True)
    fade = jnp.exp2(acc[0:8, :] - high)
    out[...] = jnp.zeros_like(out)
    out[0:1, :] = high
    out[1:2, :] = (acc[8:16, :] * fade).sum(axis=0, keepdims=True)
    out[2:3, :] = (acc[16:24, :] * fade).sum(axis=0, keepdims=True)


def source_grads_kernel(scalars, own, other, mine, theirs, logits, prods, *refs):
    outs, (lows, shift, delta, key_acc, value_acc) = refs[:SIDE], refs[SIDE:]
    for tile in range(TILES):
        lanes = slice(tile * TILE, (tile + 1) * TILE)
        a = mine[:, lanes]
        b = pltpu.roll(theirs[:, lanes], HALF, 1)
        high = jnp.maximum(a[0:1], b[0:1])
        wa = jnp.exp2(a[0:1] - high)
        wb = jnp.exp2(b[0:1] - high)
        total = a[1:2] * wa + b[1:2] * wb
        mixed = a[2:3] * wa + b[2:3] * wb
        shift[0:1, lanes] = high + jnp.log2(total)
        delta[0:1, lanes] = mixed / total
    for level in range(SIDE):
        key_acc[...] = jnp.zeros_like(key_acc)
        value_acc[...] = jnp.zeros_like(value_acc)

        def unit_grads(count, unit, carry):
            x = unit_rows(own, other, unit, QUERY)
            g = unit_rows(own, other, unit, GRAD)
            key_sum = value_sum = 0.0
            for begin in range(0, WIDE, PART):
                lanes = pl.ds(pl.multiple_of(unit * WIDE + begin, PART), PART)
                x_part = x[begin : begin + PART]
                g_part = g[begin : begin + PART]
                columns = slice(begin, begin + PART)
                highs = []
                parts = []
                for row in range(count):
                    place = (SIDE * level + unit, slice(row * TILE, (row + 1) * TILE), columns)
                    probs = jnp.exp2(logits[place] - shift[0:1, lanes])
                    highs.append(probs.astype(jnp.bfloat16))
                    parts.append((probs * (prods[place] - delta[0:1, lanes])).astype(jnp.bfloat16))
                low = jnp.concatenate(parts, axis=0)
                lows[SIDE * level + unit, : count * TILE, begin : begin + PART] = low
                value_sum += dot(jnp.concatenate(highs, axis=0), g_part, 1, 0)
                key_sum += dot(low, x_part, 1, 0)
            key_acc[: count * TILE] += key_sum
            value_acc[: count * TILE] += value_sum
            return carry

        for_units(scalars, level, unit_grads)
        for row in range(SIDE):
            for index, out in enumerate(outs):
                begin = row * TILE + index * PIECE
                rows = slice(begin, begin + PIECE)
                tile = SIDE * level + row
                out[tile, 0:PIECE, :] = (key_acc[rows, :] * SCALE).astype(jnp.bfloat16)
                out[tile, PIECE : 2 * PIECE, :] = value_acc[rows, :].astype(jnp.bfloat16)


def query_grads_kernel(scalars, kv0, kv1, kv2, kv3, lows, keep, send, acc):
    kvs = (kv0, kv1, kv2, kv3)
    acc[...] = jnp.zeros_like(acc)
    for level in range(SIDE):

        def unit_grads(count, unit, carry):
            low = lows[SIDE * level + unit, : count * TILE]
            acc[unit_lanes(unit), :] += dot(low, source_rows(kvs, level, 0, count), 0, 0)
            return carry

        for_units(scalars, level, unit_grads)
    for unit in range(SIDE):
        for level in range(SIDE):
            begin = (SIDE * unit + level) * TILE
            tile = SIDE * level + unit
            keep[tile] = acc[begin : begin + HALF, :] * SCALE
            send[tile] = (acc[begin + HALF : begin + TILE, :] * SCALE).astype(jnp.bfloat16)


def pack_kernel(sums, keep, returned, out):
    out[:, : 2 * PIECE, :] = sums[...]
    out[:, 2 * PIECE :, :] = (keep[...] + returned[...].astype(jnp.float32)).astype(jnp.bfloat16)


SMEM = pl.BlockSpec(memory_space=pltpu.SMEM)
VMEM = pl.BlockSpec(memory_space=pltpu.VMEM)
PARAMS = pltpu.CompilerParams(vmem_limit_bytes=LIMIT)


def cost(dots):
    flops = 10 * dots * 2 * WIDE * WIDE * DIM
    return pl.CostEstimate(flops=flops, bytes_accessed=2**20, transcendentals=0)


def row_stats(scalars, lim, own, other, kvs):
    operands = (scalars, lim, own, other, *kvs)
    return pl.pallas_call(
        stats_kernel,
        out_shape=[jax.ShapeDtypeStruct((8, ROWS), jnp.float32)]
        + [jax.ShapeDtypeStruct((TILES, WIDE, WIDE), jnp.float32)] * 2,
        in_specs=[SMEM] + [VMEM] * (len(operands) - 1),
        out_specs=[VMEM] * 3,
        scratch_shapes=[pltpu.VMEM((24, ROWS), jnp.float32)],
        compiler_params=PARAMS,
        cost_estimate=cost(4),
        name="stats",
    )(*operands)


def source_grads(*operands):
    piece = jax.ShapeDtypeStruct((TILES, 2 * PIECE, DIM), jnp.bfloat16)
    lows = jax.ShapeDtypeStruct((TILES, WIDE, WIDE), jnp.bfloat16)
    return pl.pallas_call(
        source_grads_kernel,
        out_shape=[piece] * SIDE + [lows],
        in_specs=[SMEM] + [VMEM] * (len(operands) - 1),
        out_specs=[VMEM] * (SIDE + 1),
        scratch_shapes=[
            pltpu.VMEM((8, ROWS), jnp.float32),
            pltpu.VMEM((8, ROWS), jnp.float32),
            pltpu.VMEM((WIDE, DIM), jnp.float32),
            pltpu.VMEM((WIDE, DIM), jnp.float32),
        ],
        compiler_params=PARAMS,
        cost_estimate=cost(4),
        name="source_grads",
    )(*operands)


def query_grads(scalars, kvs, lows):
    shape = (TILES, HALF, DIM)
    return pl.pallas_call(
        query_grads_kernel,
        out_shape=[jax.ShapeDtypeStruct(shape, jnp.float32), jax.ShapeDtypeStruct(shape, jnp.bfloat16)],
        in_specs=[SMEM] + [VMEM] * 5,
        out_specs=[VMEM] * 2,
        scratch_shapes=[pltpu.VMEM((ROWS, DIM), jnp.float32)],
        compiler_params=PARAMS,
        cost_estimate=cost(1),
        name="query_grads",
    )(scalars, *kvs, lows)


def pack_result(sums, keep, returned):
    return pl.pallas_call(
        pack_kernel,
        out_shape=jax.ShapeDtypeStruct((TILES, 2 * PIECE + HALF, DIM), jnp.bfloat16),
        in_specs=[VMEM] * 3,
        out_specs=VMEM,
        compiler_params=PARAMS,
        name="pack",
    )(sums, keep, returned)


def by_head_kernel(*refs):
    out = refs[-1]
    low = 0
    for ref in refs[:-1]:
        high = low + ref.shape[0]
        for tile in range(TILES):
            wide = ref.shape[1] > DIM
            out[tile, low:high, :] = ref[:, tile * DIM : (tile + 1) * DIM] if wide else ref[...]
        low = high


def by_head(*arrays):
    rows = sum(a.shape[0] for a in arrays)
    return pl.pallas_call(
        by_head_kernel,
        out_shape=jax.ShapeDtypeStruct((TILES, rows, DIM), jnp.bfloat16),
        in_specs=[VMEM] * len(arrays),
        out_specs=VMEM,
        name="by_head",
    )(*arrays)


def by_row_kernel(heads, keys, values, queries):
    for tile in range(TILES):
        columns = slice(tile * DIM, (tile + 1) * DIM)
        keys[:, columns] = heads[tile, :PIECE, :]
        values[:, columns] = heads[tile, PIECE : 2 * PIECE, :]
        queries[:, columns] = heads[tile, 2 * PIECE :, :]


def by_row(heads):
    rows = (PIECE, PIECE, HALF)
    return pl.pallas_call(
        by_row_kernel,
        out_shape=[jax.ShapeDtypeStruct((n, TILES * DIM), jnp.bfloat16) for n in rows],
        in_specs=[VMEM],
        out_specs=[VMEM] * 3,
        compiler_params=PARAMS,
        name="by_row",
    )(heads)


def device(row, column, level, core):
    return (row * SIDE + column) * 2 * SIDE + level * 2 + core


GROUPS = [
    [device(row, column, level, core) for level in range(SIDE) for row in range(SIDE)]
    for column in range(SIDE)
    for core in range(2)
]


def exchange(a):
    return lax.all_to_all(a, ("tgt", "src"), 0, 0, axis_index_groups=GROUPS, tiled=True)


def swap_cores(a):
    return lax.ppermute(a, "src", [(i, i ^ 1) for i in range(2 * SIDE)])


def along(a, shift):
    def target(i):
        return i - i % SIDE + (i + shift) % SIDE

    return lax.ppermute(a, "tgt", [(i, target(i)) for i in range(TILES)])


def shards(queries, keys, values, out_grad, read_points, block_mask):
    place = lax.axis_index("src")
    level, core = place // 2, place % 2
    column = lax.axis_index("tgt") % SIDE

    reads = lax.dynamic_slice_in_dim(read_points, level * TILE, TILE)
    digits = jnp.stack([reads // 64, reads % 64]).astype(jnp.bfloat16)
    flags = block_mask.reshape(SIDE, SIDE, SIDE, SIDE, 2, SIDE)
    flags = lax.dynamic_index_in_dim(flags, column, 1, False)
    flags = lax.dynamic_index_in_dim(flags, core, 3, False).transpose(2, 3, 0, 1)
    digits = jnp.pad(digits, ((0, 14), (0, 0)))
    digits, flags = lax.optimization_barrier((digits, flags))
    kv = exchange(by_head(keys, values))
    kvs = [kv] + [along(kv, k) for k in (1, 3, 2)]
    own = exchange(by_head(queries, out_grad, digits))
    other = swap_cores(own)

    reads = own[:, DIGIT].astype(jnp.int32) * 64 + own[:, DIGIT + 1].astype(jnp.int32)
    begins = (
        jnp.arange(SIDE, dtype=jnp.int32)[:, None] * (2 * WIDE)
        + core * WIDE
        + jnp.arange(SIDE, dtype=jnp.int32)[None, :] * TILE
    )
    tops = reads[TILES - SIDE :, -1]
    first = jnp.sum(tops[None, :] <= begins[:, :1], axis=1)
    whole = jnp.sum(tops[None, :] <= begins[:, 1:2], axis=1)
    offsets = jnp.stack([(column - k) % SIDE * PIECE for k in (0, 1, 3, 2)])
    scalars = jnp.concatenate([first, offsets, whole]).astype(jnp.int32)
    ordered = jnp.where(core == 0, reads, jnp.roll(reads, HALF, axis=1))
    ordered = ordered.reshape(SIDE, SIDE, TILE).transpose(1, 0, 2)
    lim = jnp.where(flags[..., None] == 1, ordered[None, None], 0) - begins[:, :, None, None, None]
    lim = lim.reshape(TILES, ROWS)

    mine, logits, prods = row_stats(scalars, lim, own, other, kvs)
    theirs = swap_cores(mine)
    part0, part1, part2, part3, lows = source_grads(
        scalars, own, other, mine, theirs, logits, prods
    )
    got3, got1, got2 = along(part3, 2), along(part1, 3), along(part2, 1)
    keep, send = query_grads(scalars, kvs, lows)
    returned = swap_cores(send)
    sums = functools.reduce(jnp.add, [p.astype(jnp.float32) for p in (part0, got1, got2, got3)])
    result = pack_result(sums.astype(jnp.bfloat16), keep, returned)
    key_grad, value_grad, query_grad = by_row(exchange(result))
    return query_grad, key_grad, value_grad


def solution(mesh):
    in_specs = (
        P(("tgt", "src"), "head"),
        P(("src", "tgt"), "head"),
        P(("src", "tgt"), "head"),
        P(("tgt", "src"), "head"),
        P("tgt"),
        P(),
    )
    out_specs = (P(("tgt", "src"), "head"), P(("src", "tgt"), "head"), P(("src", "tgt"), "head"))
    return jax.shard_map(shards, mesh=mesh, in_specs=in_specs, out_specs=out_specs, check_vma=False)
```

```python
import functools

import jax
import jax.numpy as jnp
from jax import lax
from jax.experimental import pallas as pl
from jax.experimental.pallas import tpu as pltpu
from jax.sharding import PartitionSpec as P

DIM = 128
TILE = 128
SIDE = 4
TILES = SIDE * SIDE
WIDE = SIDE * TILE
PART = WIDE // 2
ROWS = TILES * TILE
HALF = TILE // 2
PIECE = 32
QUERY = 0
GRAD = QUERY + HALF
DIGIT = GRAD + HALF
MASKED = -1e30
FLOOR = -1e29
SCALE = float(DIM) ** -0.5
LOG2E = 1.4426950408889634
LIMIT = 4 * 1024 * 1024


def dot(a, b, left, right):
    dims = (((left,), (right,)), ((), ()))
    return lax.dot_general(a, b, dims, preferred_element_type=jnp.float32)


def unit_rows(own, other, unit, low):
    parts = []
    for level in range(SIDE):
        for ref in (own, other):
            parts.append(ref[SIDE * level + unit, low : low + HALF, :])
    return jnp.concatenate(parts, axis=0)


def source_rows(kvs, level, low, count=SIDE):
    parts = []
    for row in range(count):
        for kv in kvs:
            parts.append(kv[SIDE * level + row, low : low + PIECE, :])
    return jnp.concatenate(parts, axis=0)


def source_steps(scalars):
    step = lax.broadcasted_iota(jnp.int32, (PIECE, WIDE), 0)
    return jnp.concatenate([step + scalars[SIDE + chunk] for chunk in range(SIDE)], axis=0)


def masked(block, steps, lim, level, row, lanes):
    part = block[row * TILE : (row + 1) * TILE]
    return jnp.where(steps < lim[SIDE * level + row, lanes][None, :], part, MASKED)


def unit_lanes(unit):
    return pl.ds(pl.multiple_of(unit * WIDE, WIDE), WIDE)


def for_units(scalars, level, body):
    first, whole = scalars[level], scalars[2 * SIDE + level]
    lax.fori_loop(first, whole, functools.partial(body, 1), 0)
    lax.fori_loop(whole, SIDE, functools.partial(body, SIDE), 0)


def stats_kernel(scalars, lim, own, other, kv0, kv1, kv2, kv3, out, logits, prods, acc):
    kvs = (kv0, kv1, kv2, kv3)
    acc[...] = jnp.zeros_like(acc)
    acc[0:8, :] = jnp.full((8, ROWS), MASKED, jnp.float32)
    for level in range(SIDE):

        def unit_stats(count, unit, carry):
            lanes = unit_lanes(unit)
            steps = source_steps(scalars)
            x = unit_rows(own, other, unit, QUERY)
            g = unit_rows(own, other, unit, GRAD)
            product = dot(source_rows(kvs, level, 0, count), x, 1, 1)
            mixture = dot(source_rows(kvs, level, PIECE, count), g, 1, 1)
            high = acc[0:8, lanes]
            total = acc[8:16, lanes]
            mixed = acc[16:24, lanes]
            shape = (TILE // 8, 8, WIDE)
            for row in range(count):
                rows = slice(row * TILE, (row + 1) * TILE)
                block = masked(product, steps, lim, level, row, lanes) * (SCALE * LOG2E)
                logits[SIDE * level + unit, rows] = block
                prods[SIDE * level + unit, rows] = mixture[rows]
                top = jnp.maximum(high, block.reshape(shape).max(axis=0))
                base = jnp.maximum(top, FLOOR)
                weights = jnp.exp2(block.reshape(shape) - base[None])
                fade = jnp.exp2(high - top)
                total = total * fade + weights.sum(axis=0)
                mixed = mixed * fade + (weights * mixture[rows].reshape(shape)).sum(axis=0)
                high = top
            acc[0:8, lanes] = high
            acc[8:16, lanes] = total
            acc[16:24, lanes] = mixed
            return carry

        for_units(scalars, level, unit_stats)
    high = acc[0:8, :].max(axis=0, keepdims=True)
    fade = jnp.exp2(acc[0:8, :] - high)
    out[...] = jnp.zeros_like(out)
    out[0:1, :] = high
    out[1:2, :] = (acc[8:16, :] * fade).sum(axis=0, keepdims=True)
    out[2:3, :] = (acc[16:24, :] * fade).sum(axis=0, keepdims=True)


def source_grads_kernel(scalars, own, other, mine, theirs, logits, prods, *refs):
    outs, (lows, shift, delta, key_acc, value_acc) = refs[:SIDE], refs[SIDE:]
    for tile in range(TILES):
        lanes = slice(tile * TILE, (tile + 1) * TILE)
        a = mine[:, lanes]
        b = pltpu.roll(theirs[:, lanes], HALF, 1)
        high = jnp.maximum(a[0:1], b[0:1])
        wa = jnp.exp2(a[0:1] - high)
        wb = jnp.exp2(b[0:1] - high)
        total = a[1:2] * wa + b[1:2] * wb
        mixed = a[2:3] * wa + b[2:3] * wb
        shift[0:1, lanes] = high + jnp.log2(total)
        delta[0:1, lanes] = mixed / total
    for level in range(SIDE):
        key_acc[...] = jnp.zeros_like(key_acc)
        value_acc[...] = jnp.zeros_like(value_acc)

        def unit_grads(count, unit, carry):
            x = unit_rows(own, other, unit, QUERY)
            g = unit_rows(own, other, unit, GRAD)
            key_sum = value_sum = 0.0
            for begin in range(0, WIDE, PART):
                lanes = pl.ds(pl.multiple_of(unit * WIDE + begin, PART), PART)
                x_part = x[begin : begin + PART]
                g_part = g[begin : begin + PART]
                columns = slice(begin, begin + PART)
                highs = []
                parts = []
                for row in range(count):
                    place = (SIDE * level + unit, slice(row * TILE, (row + 1) * TILE), columns)
                    probs = jnp.exp2(logits[place] - shift[0:1, lanes])
                    highs.append(probs.astype(jnp.bfloat16))
                    parts.append((probs * (prods[place] - delta[0:1, lanes])).astype(jnp.bfloat16))
                low = jnp.concatenate(parts, axis=0)
                lows[SIDE * level + unit, : count * TILE, begin : begin + PART] = low
                value_sum += dot(jnp.concatenate(highs, axis=0), g_part, 1, 0)
                key_sum += dot(low, x_part, 1, 0)
            key_acc[: count * TILE] += key_sum
            value_acc[: count * TILE] += value_sum
            return carry

        for_units(scalars, level, unit_grads)
        for row in range(SIDE):
            for index, out in enumerate(outs):
                begin = row * TILE + index * PIECE
                rows = slice(begin, begin + PIECE)
                tile = SIDE * level + row
                out[tile, 0:PIECE, :] = (key_acc[rows, :] * SCALE).astype(jnp.bfloat16)
                out[tile, PIECE : 2 * PIECE, :] = value_acc[rows, :].astype(jnp.bfloat16)


def query_grads_kernel(scalars, kv0, kv1, kv2, kv3, lows, keep, send, acc):
    kvs = (kv0, kv1, kv2, kv3)
    acc[...] = jnp.zeros_like(acc)
    for level in range(SIDE):

        def unit_grads(count, unit, carry):
            low = lows[SIDE * level + unit, : count * TILE]
            acc[unit_lanes(unit), :] += dot(low, source_rows(kvs, level, 0, count), 0, 0)
            return carry

        for_units(scalars, level, unit_grads)
    for unit in range(SIDE):
        for level in range(SIDE):
            begin = (SIDE * unit + level) * TILE
            tile = SIDE * level + unit
            keep[tile] = acc[begin : begin + HALF, :] * SCALE
            send[tile] = (acc[begin + HALF : begin + TILE, :] * SCALE).astype(jnp.bfloat16)


def pack_kernel(part0, part1, part2, part3, keep, returned, out):
    sums = part0[...].astype(jnp.float32)
    for part in (part1, part2, part3):
        sums += part[...].astype(jnp.float32)
    out[:, : 2 * PIECE, :] = sums.astype(jnp.bfloat16)
    out[:, 2 * PIECE :, :] = (keep[...] + returned[...].astype(jnp.float32)).astype(jnp.bfloat16)


SMEM = pl.BlockSpec(memory_space=pltpu.SMEM)
VMEM = pl.BlockSpec(memory_space=pltpu.VMEM)
PARAMS = pltpu.CompilerParams(vmem_limit_bytes=LIMIT)


def cost(dots):
    flops = 10 * dots * 2 * WIDE * WIDE * DIM
    return pl.CostEstimate(flops=flops, bytes_accessed=2**20, transcendentals=0)


def row_stats(scalars, lim, own, other, kvs):
    operands = (scalars, lim, own, other, *kvs)
    return pl.pallas_call(
        stats_kernel,
        out_shape=[jax.ShapeDtypeStruct((8, ROWS), jnp.float32)]
        + [jax.ShapeDtypeStruct((TILES, WIDE, WIDE), jnp.float32)] * 2,
        in_specs=[SMEM] + [VMEM] * (len(operands) - 1),
        out_specs=[VMEM] * 3,
        scratch_shapes=[pltpu.VMEM((24, ROWS), jnp.float32)],
        compiler_params=PARAMS,
        cost_estimate=cost(4),
        name="stats",
    )(*operands)


def source_grads(*operands):
    piece = jax.ShapeDtypeStruct((TILES, 2 * PIECE, DIM), jnp.bfloat16)
    lows = jax.ShapeDtypeStruct((TILES, WIDE, WIDE), jnp.bfloat16)
    return pl.pallas_call(
        source_grads_kernel,
        out_shape=[piece] * SIDE + [lows],
        in_specs=[SMEM] + [VMEM] * (len(operands) - 1),
        out_specs=[VMEM] * (SIDE + 1),
        scratch_shapes=[
            pltpu.VMEM((8, ROWS), jnp.float32),
            pltpu.VMEM((8, ROWS), jnp.float32),
            pltpu.VMEM((WIDE, DIM), jnp.float32),
            pltpu.VMEM((WIDE, DIM), jnp.float32),
        ],
        compiler_params=PARAMS,
        cost_estimate=cost(4),
        name="source_grads",
    )(*operands)


def query_grads(scalars, kvs, lows):
    shape = (TILES, HALF, DIM)
    return pl.pallas_call(
        query_grads_kernel,
        out_shape=[jax.ShapeDtypeStruct(shape, jnp.float32), jax.ShapeDtypeStruct(shape, jnp.bfloat16)],
        in_specs=[SMEM] + [VMEM] * 5,
        out_specs=[VMEM] * 2,
        scratch_shapes=[pltpu.VMEM((ROWS, DIM), jnp.float32)],
        compiler_params=PARAMS,
        cost_estimate=cost(1),
        name="query_grads",
    )(scalars, *kvs, lows)


def pack_result(*operands):
    return pl.pallas_call(
        pack_kernel,
        out_shape=jax.ShapeDtypeStruct((TILES, 2 * PIECE + HALF, DIM), jnp.bfloat16),
        in_specs=[VMEM] * 6,
        out_specs=VMEM,
        compiler_params=PARAMS,
        name="pack",
    )(*operands)


def by_head_kernel(*refs):
    out = refs[-1]
    low = 0
    for ref in refs[:-1]:
        high = low + ref.shape[0]
        for tile in range(TILES):
            wide = ref.shape[1] > DIM
            out[tile, low:high, :] = ref[:, tile * DIM : (tile + 1) * DIM] if wide else ref[...]
        low = high


def by_head(*arrays):
    rows = sum(a.shape[0] for a in arrays)
    return pl.pallas_call(
        by_head_kernel,
        out_shape=jax.ShapeDtypeStruct((TILES, rows, DIM), jnp.bfloat16),
        in_specs=[VMEM] * len(arrays),
        out_specs=VMEM,
        name="by_head",
    )(*arrays)


def by_row_kernel(heads, keys, values, queries):
    for tile in range(TILES):
        columns = slice(tile * DIM, (tile + 1) * DIM)
        keys[:, columns] = heads[tile, :PIECE, :]
        values[:, columns] = heads[tile, PIECE : 2 * PIECE, :]
        queries[:, columns] = heads[tile, 2 * PIECE :, :]


def by_row(heads):
    rows = (PIECE, PIECE, HALF)
    return pl.pallas_call(
        by_row_kernel,
        out_shape=[jax.ShapeDtypeStruct((n, TILES * DIM), jnp.bfloat16) for n in rows],
        in_specs=[VMEM],
        out_specs=[VMEM] * 3,
        compiler_params=PARAMS,
        name="by_row",
    )(heads)


def device(row, column, level, core):
    return (row * SIDE + column) * 2 * SIDE + level * 2 + core


GROUPS = [
    [device(row, column, level, core) for level in range(SIDE) for row in range(SIDE)]
    for column in range(SIDE)
    for core in range(2)
]


def exchange(a):
    return lax.all_to_all(a, ("tgt", "src"), 0, 0, axis_index_groups=GROUPS, tiled=True)


def swap_cores(a):
    return lax.ppermute(a, "src", [(i, i ^ 1) for i in range(2 * SIDE)])


def along(a, shift):
    def target(i):
        return i - i % SIDE + (i + shift) % SIDE

    return lax.ppermute(a, "tgt", [(i, target(i)) for i in range(TILES)])


def shards(queries, keys, values, out_grad, read_points, block_mask):
    place = lax.axis_index("src")
    level, core = place // 2, place % 2
    column = lax.axis_index("tgt") % SIDE

    reads = lax.dynamic_slice_in_dim(read_points, level * TILE, TILE)
    digits = jnp.stack([reads // 64, reads % 64]).astype(jnp.bfloat16)
    flags = block_mask.reshape(SIDE, SIDE, SIDE, SIDE, 2, SIDE)
    flags = lax.dynamic_index_in_dim(flags, column, 1, False)
    flags = lax.dynamic_index_in_dim(flags, core, 3, False).transpose(2, 3, 0, 1)
    digits = jnp.pad(digits, ((0, 14), (0, 0)))
    digits, flags = lax.optimization_barrier((digits, flags))
    kv = exchange(by_head(keys, values))
    kvs = [kv] + [along(kv, k) for k in (1, 3, 2)]
    own = exchange(by_head(queries, out_grad, digits))
    other = swap_cores(own)

    reads = own[:, DIGIT].astype(jnp.int32) * 64 + own[:, DIGIT + 1].astype(jnp.int32)
    begins = (
        jnp.arange(SIDE, dtype=jnp.int32)[:, None] * (2 * WIDE)
        + core * WIDE
        + jnp.arange(SIDE, dtype=jnp.int32)[None, :] * TILE
    )
    tops = reads[TILES - SIDE :, -1]
    first = jnp.sum(tops[None, :] <= begins[:, :1], axis=1)
    whole = jnp.sum(tops[None, :] <= begins[:, 1:2], axis=1)
    offsets = jnp.stack([(column - k) % SIDE * PIECE for k in (0, 1, 3, 2)])
    scalars = jnp.concatenate([first, offsets, whole]).astype(jnp.int32)
    ordered = jnp.where(core == 0, reads, jnp.roll(reads, HALF, axis=1))
    ordered = ordered.reshape(SIDE, SIDE, TILE).transpose(1, 0, 2)
    lim = jnp.where(flags[..., None] == 1, ordered[None, None], 0) - begins[:, :, None, None, None]
    lim = lim.reshape(TILES, ROWS)

    mine, logits, prods = row_stats(scalars, lim, own, other, kvs)
    theirs = swap_cores(mine)
    part0, part1, part2, part3, lows = source_grads(
        scalars, own, other, mine, theirs, logits, prods
    )
    got3, got1, got2 = along(part3, 2), along(part1, 3), along(part2, 1)
    keep, send = query_grads(scalars, kvs, lows)
    returned = swap_cores(send)
    result = pack_result(part0, got1, got2, got3, keep, returned)
    key_grad, value_grad, query_grad = by_row(exchange(result))
    return query_grad, key_grad, value_grad


def solution(mesh):
    in_specs = (
        P(("tgt", "src"), "head"),
        P(("src", "tgt"), "head"),
        P(("src", "tgt"), "head"),
        P(("tgt", "src"), "head"),
        P("tgt"),
        P(),
    )
    out_specs = (P(("tgt", "src"), "head"), P(("src", "tgt"), "head"), P(("src", "tgt"), "head"))
    return jax.shard_map(shards, mesh=mesh, in_specs=in_specs, out_specs=out_specs, check_vma=False)
```
